512 devices in a mesh: chan: 16 (over y, core), blk: 32 (over z, x).
Axes of the slice: x: 4, y: 8, z: 8, core: 2. Of those that a mesh axis runs over, the one named last changes fastest.
Arguments:
- comp_alms: float32 [3, 4, 32, 4096], P(None, None, 'blk', 'chan'), may hold values from -6 to 6
- legendre: bfloat16 [2, 32, 4096, 128], P(None, 'blk'), may hold values from -0.09375 to 0.09375
- inv_noise: float32 [16, 2, 128, 8192], P('chan', None, 'blk'), may hold values from 0.5 to 5
- beam_window: float32 [16, 4096], replicated, may hold values from 0.1 to 1
- mixing: float32 [16, 3], replicated, may hold values from 0.2 to 1.5
- channel_of: int32 [16], replicated, may hold values from 0 to 15, each once
- m_orders: int32 [32], replicated, may hold values from 0 to 4095, as said below
- cycle_of: int32 [128], replicated, may hold values from 0 to 127, each once
- cycle_pixels: int32 [128], replicated, may hold values from 4 to 8192, as said below
Outputs:
- normal_product: float32 [3, 4, 32, 4096], P(None, None, 'blk', 'chan')
The draws below stay inside these ranges and needn't reach their ends.
Inputs may be any that keep to these rules, and one draw needn't show every extreme that they name: `m_orders`: the orders are distinct. `cycle_pixels`: each entry is 4 * min(h, 2048, 8192 - h) for some cycle number h of 1 to 8191; at least one entry equals 8192.
All inputs are finite; a program needn't handle non-finite values.
Results may differ from the reference program's by a relative error of at most 0.0022.
Values may be sent and summed in bfloat16 or wider, within the bound.
No kernel may reach another device: no remote copies, remote signals or barrier semaphores. Data moves between devices by JAX's collectives and lax.ppermute only.
A program may use at most 128 MiB of HBM per device.

```python
import math
import jax
import jax.numpy as jnp
from jax import lax

L = 4096
PIX = 8192
NC = 3
CH = 16
M_TOT = 32
R_TOT = 128


def draw_m_orders(key, part):
    return jax.random.permutation(key, L)[:M_TOT].astype(jnp.int32)


def draw_cycle_pixels(key, part):
    first_key, second_key = jax.random.split(jax.random.fold_in(key, 17))
    numbers = jax.random.randint(first_key, (R_TOT,), 1, PIX).astype(jnp.int32)
    position = jax.random.randint(second_key, (), 0, R_TOT)
    numbers = numbers.at[position].set(PIX // 2)
    quarter = PIX // 4
    return (4 * jnp.minimum(jnp.minimum(numbers, quarter), PIX - numbers)).astype(jnp.int32)


def level_of(stream_key, extent, shards, least, high):
    gain = 1.0
    for dim, shards_of in shards:
        heights = jax.random.uniform(jax.random.fold_in(jax.random.fold_in(stream_key, 6), dim), (shards_of,), jnp.float32, least / len(shards), high / len(shards))
        gain = gain * jnp.repeat(jnp.exp(heights), extent[dim] // shards_of).reshape((-1,) + (1,) * (len(extent) - 1 - dim))
    return gain


def normal_values(rng, dims, deviation, bound, cuts=(), held_as=jnp.bfloat16):
    factor_of = level_of(rng, dims, cuts, -0.22, 0.18) if cuts else 1.0
    result = jax.random.normal(rng, dims, jnp.float32) * deviation * factor_of
    return jnp.minimum(jnp.maximum(result, -bound), bound).astype(held_as)


def setup_inputs(seed: int = 0) -> dict:
    key_list = jax.random.split(jax.random.key(seed), 10)
    comp_alms = normal_values(key_list[0], (NC, 4, M_TOT, L), 1.0, 6.0, ((2, 32), (3, 16)), jnp.float32)
    legendre = normal_values(key_list[1], (2, M_TOT, L, R_TOT), L ** -0.5, 0.09375, ((1, 32),))
    inv_noise = jnp.clip(jnp.exp(math.log(5.0) - 2.3025851 * jax.random.uniform(key_list[2], (CH, 2, R_TOT, PIX), jnp.float32) ** level_of(key_list[2], (CH, 2, R_TOT, PIX), ((0, 16), (2, 32)), -0.2, 0.2)), 0.5, 5.0)
    beam_window = jnp.clip(jax.random.uniform(key_list[3], (CH, L), jnp.float32, 0.1, 1.0), 0.1, 1.0)
    mixing = jnp.clip(jax.random.uniform(key_list[4], (CH, NC), jnp.float32, 0.2, 1.5), 0.2, 1.5)
    channel_of = jax.random.permutation(key_list[5], CH).astype(jnp.int32)
    m_orders = draw_m_orders(jax.random.fold_in(key_list[9], 71), 0)
    cycle_of = jax.random.permutation(key_list[7], R_TOT).astype(jnp.int32)
    cycle_pixels = draw_cycle_pixels(jax.random.fold_in(key_list[9], 71), 0)
    return {"comp_alms": comp_alms, "legendre": legendre, "inv_noise": inv_noise, "beam_window": beam_window, "mixing": mixing, "channel_of": channel_of, "m_orders": m_orders, "cycle_of": cycle_of, "cycle_pixels": cycle_pixels}


def phase_rows(orders, pix_count, cycle_width):
    columns = jnp.arange(cycle_width, dtype=jnp.int32)
    phase_steps = (orders[:, None] * (2 * columns[None, :] + 1)) % (2 * pix_count)
    angles = phase_steps.astype(jnp.float32) * (jnp.float32(math.pi) / pix_count.astype(jnp.float32))
    return jnp.concatenate([jnp.cos(angles), jnp.sin(angles)], axis=0).astype(jnp.bfloat16)


def combine_forward(plus_sum, minus_sum):
    return jnp.stack([plus_sum[:, 0] - minus_sum[:, 3], plus_sum[:, 1] + minus_sum[:, 2],
                      plus_sum[:, 2] + minus_sum[:, 1], plus_sum[:, 3] - minus_sum[:, 0]], axis=1)


def twist_grads(cycle_grads):
    return jnp.stack([-cycle_grads[:, 3], cycle_grads[:, 2], cycle_grads[:, 1], -cycle_grads[:, 0]], axis=1)


def cycle_work(coeffs, weights, orders, pix_count):
    slots = coeffs.shape[0]
    cycle_width = weights.shape[-1]
    phases = phase_rows(orders, pix_count, cycle_width)
    half_rows = phases.shape[0] // 2
    real_part = coeffs[:, 0::2]
    imag_part = coeffs[:, 1::2]
    stacked = jnp.concatenate([real_part, -imag_part], axis=2).reshape(2 * slots, 2 * half_rows)
    maps = jnp.dot(stacked, phases, preferred_element_type=jnp.float32)
    live_mask = jnp.arange(cycle_width, dtype=jnp.int32) < pix_count
    scaled = jnp.where(live_mask[None, None, :], weights, 0.0) / pix_count.astype(jnp.float32)
    weighted = (scaled.reshape(maps.shape) * maps).astype(jnp.bfloat16)
    returned = lax.dot_general(weighted, phases, (((1,), (1,)), ((), ())), preferred_element_type=jnp.float32)
    grad_real = returned[:, :half_rows].reshape(slots, 2, half_rows)
    grad_imag = (-returned[:, half_rows:]).reshape(slots, 2, half_rows)
    return jnp.stack([grad_real, grad_imag], axis=2).reshape(slots, 4, half_rows).astype(jnp.bfloat16)


def mix_components(mix_rows, components):
    accum = mix_rows[:, 0, None, None, None] * components[0][None]
    for comp_index in range(1, components.shape[0]):
        accum = accum + mix_rows[:, comp_index, None, None, None] * components[comp_index][None]
    return accum


def reference(comp_alms, legendre, inv_noise, beam_window, mixing, channel_of, m_orders, cycle_of, cycle_pixels):
    length = legendre.shape[2]
    cycle_total = legendre.shape[3]
    mix_rows = jnp.take(mixing, channel_of, axis=0)
    beam_rows = jnp.take(beam_window, channel_of, axis=0)
    keep_mask = (jnp.arange(length, dtype=jnp.int32)[None, :] >= m_orders[:, None]).astype(jnp.float32)
    mixed_alm = mix_components(mix_rows, comp_alms)
    chan_alm = (mixed_alm * beam_rows[:, None, None, :] * keep_mask[None, None]).astype(jnp.bfloat16)
    channels = chan_alm.shape[0]

    def forward_order(index):
        tables = lax.dynamic_index_in_dim(legendre, index, 1, keepdims=False)
        row_block = lax.dynamic_index_in_dim(chan_alm, index, 2, keepdims=False).reshape(channels * 4, length)
        plus_sum = jnp.dot(row_block, tables[0], preferred_element_type=jnp.float32).reshape(channels, 4, cycle_total)
        minus_sum = jnp.dot(row_block, tables[1], preferred_element_type=jnp.float32).reshape(channels, 4, cycle_total)
        return combine_forward(plus_sum, minus_sum)

    cycle_coeffs = lax.map(forward_order, jnp.arange(M_TOT, dtype=jnp.int32))
    cycle_coeffs = jnp.transpose(cycle_coeffs, (1, 2, 0, 3)).astype(jnp.bfloat16)
    slot_coeffs = jnp.take(cycle_coeffs, cycle_of, axis=3)

    def per_cycle(slot):
        coeffs = lax.dynamic_index_in_dim(slot_coeffs, slot, 3, keepdims=False)
        weights = lax.dynamic_index_in_dim(inv_noise, slot, 2, keepdims=False)
        pix_count = cycle_pixels[cycle_of[slot]]
        return cycle_work(coeffs, weights, m_orders, pix_count)

    slot_grads = lax.map(per_cycle, jnp.arange(R_TOT, dtype=jnp.int32))
    slot_grads = jnp.transpose(slot_grads, (1, 2, 3, 0))
    cycle_grads = jnp.zeros_like(slot_grads).at[:, :, :, cycle_of].set(slot_grads)

    def adjoint_order(index):
        tables = lax.dynamic_index_in_dim(legendre, index, 1, keepdims=False)
        order_grads = lax.dynamic_index_in_dim(cycle_grads, index, 2, keepdims=False)
        twisted = twist_grads(order_grads)
        accum = lax.dot_general(order_grads.reshape(channels * 4, cycle_total), tables[0], (((1,), (1,)), ((), ())), preferred_element_type=jnp.float32)
        accum = accum + lax.dot_general(twisted.reshape(channels * 4, cycle_total), tables[1], (((1,), (1,)), ((), ())), preferred_element_type=jnp.float32)
        return accum.reshape(channels, 4, length)

    alm_grads = lax.map(adjoint_order, jnp.arange(M_TOT, dtype=jnp.int32))
    alm_grads = jnp.transpose(alm_grads, (1, 2, 0, 3)) * keep_mask[None, None]
    beamed = alm_grads * beam_rows[:, None, None, :]
    return jnp.einsum('kc,kpml->cpml', mix_rows, beamed, precision=lax.Precision.HIGHEST)
```

```python
import functools

import jax
import jax.numpy as jnp
from jax import lax
from jax.experimental import pallas as pl
from jax.experimental.pallas import tpu as pltpu
from jax.sharding import PartitionSpec as P

F32 = jnp.float32
BF16 = jnp.bfloat16
LANES = 128
NT = (((1,), (1,)), ((), ()))
TN = (((0,), (0,)), ((), ()))
NN = (((1,), (0,)), ((), ()))
COS = (0.9999999887921183, -19.739204415555925, 64.93911321613162, -85.45006149635309,
       60.16698573653733, -25.965151588112157, 6.525190124026944)
SIN = (6.28318530240345, -41.341700371179485, 81.60512965170976, -76.70298335354587,
       42.02566158843437, -14.898837201069828, 3.2367039052082127)

SMEM = pl.BlockSpec(memory_space=pltpu.SMEM)
VMEM = pl.BlockSpec(memory_space=pltpu.VMEM)
ANY = pl.BlockSpec(memory_space=pl.ANY)


def nearest(x):
    return jnp.floor(x + 0.5)


def poly(z, terms):
    total = jnp.full_like(z, terms[-1])
    for term in terms[-2::-1]:
        total = total * z + term
    return total


def cos_turns(y):
    return poly(y * y, COS)


def sin_turns(y):
    return y * poly(y * y, SIN)


def turns_of(steps, period):
    inverse = 1.0 / period
    rest = steps - nearest(steps * inverse) * period
    return rest * inverse


def forward_kernel(
    chan_of, mixing, orders, comp, beam, legendre, out, beam_s, leg_s, alm_s, sems, *, chan, blk
):
    width = comp.shape[3]
    first = chan() * width
    copies = [
        pltpu.make_async_copy(beam.at[:, pl.ds(first, width)], beam_s, sems.at[0]),
        pltpu.make_async_copy(legendre.at[0, 0, pl.ds(first, width), :], leg_s.at[pl.ds(0, width)], sems.at[1]),
        pltpu.make_async_copy(legendre.at[1, 0, pl.ds(first, width), :], leg_s.at[pl.ds(width, width)], sems.at[2]),
    ]
    for copy in copies:
        copy.start()
    order = orders[blk()]
    degrees = first + lax.broadcasted_iota(jnp.int32, (1, width), 1)
    keep = jnp.where(degrees >= order, 1.0, 0.0)
    parts = [comp[c, :, 0, :] for c in range(comp.shape[0])]
    copies[0].wait()
    for k in range(out.shape[0]):
        channel = chan_of[k]
        mixed = mixing[channel, 0] * parts[0]
        for c in range(1, len(parts)):
            mixed = mixed + mixing[channel, c] * parts[c]
        alm = mixed * beam_s[pl.ds(channel, 1), :] * keep
        twisted = jnp.concatenate([-alm[3:4], alm[2:3], alm[1:2], -alm[0:1]], axis=0)
        alm_s[4 * k : 4 * k + 4, :width] = alm
        alm_s[4 * k : 4 * k + 4, width:] = twisted
    copies[1].wait()
    copies[2].wait()
    sums = lax.dot_general(alm_s[...].astype(BF16), leg_s[...], NN, preferred_element_type=F32)
    out[...] = sums.reshape(out.shape)


def cycle_kernel(cycle_of, cycle_pixels, orders, coeffs, noise, out, *, blk, slots):
    count = orders.shape[0]
    lane = lax.broadcasted_iota(jnp.int32, (8, LANES), 1)
    order_row = jnp.zeros((8, LANES), F32)
    for i in range(count):
        order_row = jnp.where(lane // 4 == i, orders[i].astype(F32), order_row)
    m = order_row[:1]
    odd8 = lane % 2 == 1
    odd = odd8[:1]
    is_q = (lane % 4 < 2)[:1]
    sign = jnp.where(odd, -1.0, 1.0)

    def swap(x):
        up = pltpu.roll(x, LANES - 1, 1)
        down = pltpu.roll(x, 1, 1)
        return jnp.where(odd8, down, up)

    first = blk() * slots
    cycles = [cycle_of[first + r] for r in range(slots)]
    row8 = lax.broadcasted_iota(jnp.int32, (8, LANES), 0)
    chosen8 = jnp.full((8, LANES), -1, jnp.int32)
    for r in range(slots):
        chosen8 = jnp.where(row8 == r, cycles[r], chosen8)
    pick = jnp.where(lane == chosen8, 1.0, 0.0).astype(BF16)
    table = coeffs[...].reshape(4 * count, LANES)
    x = lax.dot_general(pick, table, NT, preferred_element_type=F32)
    x_sign = x * jnp.where(odd8, -1.0, 1.0)
    x_swap = swap(x)

    half = noise.shape[0] // 2
    tall = half // slots
    steps_a = lax.broadcasted_iota(jnp.int32, (tall, LANES), 0).astype(F32) * m * 32.0
    steps_b = (2 * lax.broadcasted_iota(jnp.int32, (LANES, LANES), 0) + 1).astype(F32) * m
    quarter = jnp.where(odd, 0.25, 0.0)
    pixel = (
        lax.broadcasted_iota(jnp.int32, (tall, LANES), 0) * LANES
        + lax.broadcasted_iota(jnp.int32, (tall, LANES), 1)
    )
    grads = jnp.zeros((8, LANES), F32)
    for r in range(slots):
        pixels = cycle_pixels[cycles[r]]
        number = jnp.full((1, LANES), pixels, jnp.int32).astype(F32)
        inverse = 1.0 / number
        ya = turns_of(steps_a, number * 0.25)
        ya = ya - nearest(ya)
        cos_a = cos_turns(ya)
        sin_a = sin_turns(ya)
        yb = turns_of(steps_b, number * 2.0) - quarter
        yb = yb - nearest(yb)
        phases = cos_turns(yb).astype(BF16)
        left = x_sign[r : r + 1] * cos_a - x_swap[r : r + 1] * sin_a
        left = jnp.concatenate([jnp.where(is_q, left, 0.0), jnp.where(is_q, 0.0, left)], axis=0)
        maps = lax.dot_general(left.astype(BF16), phases, NT, preferred_element_type=F32)
        live = jnp.where(pixel < pixels, inverse, 0.0)
        weights = jnp.concatenate(
            [noise[pl.ds(r, tall, stride=slots), :] * live, noise[pl.ds(half + r, tall, stride=slots), :] * live],
            axis=0,
        )
        weighted = (weights * maps).astype(BF16)
        back = lax.dot_general(weighted, phases, NN, preferred_element_type=F32)
        back = jnp.where(is_q, back[:tall], back[tall:])
        total_cos = jnp.sum(cos_a * back, axis=0, keepdims=True)
        total_sin = jnp.sum(sin_a * back, axis=0, keepdims=True)
        grad = sign * total_cos - swap(jnp.broadcast_to(total_sin, (8, LANES)))[:1]
        grads = jnp.where(row8 == r, grad, grads)
    spread = lax.dot_general(grads.astype(BF16), pick, TN, preferred_element_type=F32)
    out[...] = spread.astype(BF16).reshape(out.shape)


def adjoint_kernel(
    chan_of, mixing, orders, grads, beam, legendre, out, beam_s, leg_s, sems, *, chan, blk
):
    width = out.shape[3]
    first = chan() * width
    copies = [
        pltpu.make_async_copy(beam.at[:, pl.ds(first, width)], beam_s, sems.at[0]),
        pltpu.make_async_copy(legendre.at[0, 0, pl.ds(first, width), :], leg_s.at[0], sems.at[1]),
        pltpu.make_async_copy(legendre.at[1, 0, pl.ds(first, width), :], leg_s.at[1], sems.at[2]),
    ]
    for copy in copies:
        copy.start()
    order = orders[blk()]
    degrees = first + lax.broadcasted_iota(jnp.int32, (1, width), 1)
    keep = jnp.where(degrees >= order, 1.0, 0.0)
    slots = grads.shape[0]
    straight = grads[...].astype(F32).reshape(slots * 4, LANES)
    row = lax.broadcasted_iota(jnp.int32, straight.shape, 0) % 4
    up = pltpu.roll(straight, straight.shape[0] - 1, 0)
    down = pltpu.roll(straight, 1, 0)
    up3 = pltpu.roll(straight, straight.shape[0] - 3, 0)
    down3 = pltpu.roll(straight, 3, 0)
    twisted = jnp.where(row == 0, -up3, jnp.where(row == 1, up, jnp.where(row == 2, down, -down3)))
    for copy in copies:
        copy.wait()
    sums = lax.dot_general(straight.astype(BF16), leg_s[0], NT, preferred_element_type=F32)
    sums = sums + lax.dot_general(twisted.astype(BF16), leg_s[1], NT, preferred_element_type=F32)
    totals = [jnp.zeros((4, width), F32) for _ in range(out.shape[0])]
    for k in range(slots):
        channel = chan_of[k]
        beamed = sums[4 * k : 4 * k + 4] * (beam_s[pl.ds(channel, 1), :] * keep)
        for c in range(len(totals)):
            totals[c] = totals[c] + mixing[channel, c] * beamed
    for c in range(len(totals)):
        out[c, :, 0, :] = totals[c]


def body(
    comp_alms,
    legendre,
    inv_noise,
    beam_window,
    mixing,
    channel_of,
    m_orders,
    cycle_of,
    cycle_pixels,
    interpret=False,
    chan=lambda: lax.axis_index("chan"),
    blk=lambda: lax.axis_index("blk"),
    move=lambda x, axis: lax.all_to_all(x, axis, 0, 0, tiled=True),
):
    slots = channel_of.shape[0]
    orders = m_orders.shape[0]
    cycles = legendre.shape[3]
    width = comp_alms.shape[3]
    where = dict(chan=chan, blk=blk)
    partial = pl.pallas_call(
        functools.partial(forward_kernel, **where),
        out_shape=jax.ShapeDtypeStruct((slots, 4, cycles), F32),
        in_specs=[SMEM, SMEM, SMEM, VMEM, ANY, ANY],
        out_specs=VMEM,
        scratch_shapes=[
            pltpu.VMEM((beam_window.shape[0], width), F32),
            pltpu.VMEM((2 * width, cycles), BF16),
            pltpu.VMEM((slots * 4, 2 * width), F32),
            pltpu.SemaphoreType.DMA((3,)),
        ],
        interpret=interpret,
        name="forward",
    )(channel_of, mixing, m_orders, comp_alms, beam_window, legendre)
    pieces = move(partial, "chan")
    coeffs = jnp.sum(pieces, axis=0).astype(BF16)
    coeffs = move(jnp.broadcast_to(coeffs, (orders, 4, cycles)), "blk")
    held = inv_noise.shape[2]
    tall = inv_noise.shape[3] // LANES
    noise = inv_noise.reshape(2, held, tall, LANES).transpose(0, 2, 1, 3).reshape(2 * tall * held, LANES)
    grads = pl.pallas_call(
        functools.partial(cycle_kernel, blk=blk, slots=held),
        out_shape=jax.ShapeDtypeStruct((orders, 4, cycles), BF16),
        in_specs=[SMEM, SMEM, SMEM, VMEM, VMEM],
        out_specs=VMEM,
        interpret=interpret,
        name="cycles",
    )(cycle_of, cycle_pixels, m_orders, coeffs, noise)
    grads = jnp.sum(move(grads, "blk").astype(F32), axis=0).astype(BF16)
    grads = move(jnp.broadcast_to(grads, (slots, 4, cycles)), "chan")
    return pl.pallas_call(
        functools.partial(adjoint_kernel, **where),
        out_shape=jax.ShapeDtypeStruct(comp_alms.shape, F32),
        in_specs=[SMEM, SMEM, SMEM, VMEM, ANY, ANY],
        out_specs=VMEM,
        scratch_shapes=[
            pltpu.VMEM((beam_window.shape[0], width), F32),
            pltpu.VMEM((2, width, cycles), BF16),
            pltpu.SemaphoreType.DMA((3,)),
        ],
        interpret=interpret,
        name="adjoint",
    )(channel_of, mixing, m_orders, grads, beam_window, legendre)


def solution(mesh):
    placed = (
        P(None, None, "blk", "chan"),
        P(None, "blk", None, None),
        P("chan", None, "blk", None),
        P(),
        P(),
        P(),
        P(),
        P(),
        P(),
    )
    return jax.shard_map(
        body, mesh=mesh, in_specs=placed, out_specs=P(None, None, "blk", "chan"), check_vma=False
    )
```

```python
import functools

import jax
import jax.numpy as jnp
from jax import lax
from jax.experimental import pallas as pl
from jax.experimental.pallas import tpu as pltpu
from jax.sharding import PartitionSpec as P

F32 = jnp.float32
BF16 = jnp.bfloat16
LANES = 128
NT = (((1,), (1,)), ((), ()))
TN = (((0,), (0,)), ((), ()))
NN = (((1,), (0,)), ((), ()))
COS = (0.9999999887921183, -19.739204415555925, 64.93911321613162, -85.45006149635309,
       60.16698573653733, -25.965151588112157, 6.525190124026944)
SIN = (6.28318530240345, -41.341700371179485, 81.60512965170976, -76.70298335354587,
       42.02566158843437, -14.898837201069828, 3.2367039052082127)

SMEM = pl.BlockSpec(memory_space=pltpu.SMEM)
VMEM = pl.BlockSpec(memory_space=pltpu.VMEM)
ANY = pl.BlockSpec(memory_space=pl.ANY)


def move(x, axis):
    return lax.all_to_all(x, axis, 0, 0, tiled=True)


def in_vmem(x):
    return pltpu.with_memory_space_constraint(x, pltpu.VMEM)


def nearest(x):
    return jnp.floor(x + 0.5)


def poly(z, terms):
    total = jnp.full_like(z, terms[-1])
    for term in terms[-2::-1]:
        total = total * z + term
    return total


def cos_turns(y):
    return poly(y * y, COS)


def sin_turns(y):
    return y * poly(y * y, SIN)


def turns_of(steps, period):
    inverse = 1.0 / period
    rest = steps - nearest(steps * inverse) * period
    return rest * inverse


def forward_kernel(
    chan_of, mixing, orders, comp, beam, legendre, out, comp_s, beam_s, leg_s, alm_s, sems, *, chan, blk
):
    width = comp.shape[3]
    first = chan() * width
    copies = [
        pltpu.make_async_copy(beam.at[:, pl.ds(first, width)], beam_s, sems.at[0]),
        pltpu.make_async_copy(legendre.at[0, 0, pl.ds(first, width), :], leg_s.at[pl.ds(0, width)], sems.at[1]),
        pltpu.make_async_copy(legendre.at[1, 0, pl.ds(first, width), :], leg_s.at[pl.ds(width, width)], sems.at[2]),
        pltpu.make_async_copy(comp, comp_s, sems.at[3]),
    ]
    for copy in copies:
        copy.start()
    order = orders[blk()]
    degrees = first + lax.broadcasted_iota(jnp.int32, (1, width), 1)
    keep = jnp.where(degrees >= order, 1.0, 0.0)
    copies[3].wait()
    parts = [comp_s[c, :, 0, :] * keep for c in range(comp.shape[0])]
    copies[0].wait()
    for k in range(out.shape[0]):
        channel = chan_of[k]
        mixed = mixing[0, channel] * parts[0]
        for c in range(1, len(parts)):
            mixed = mixed + mixing[c, channel] * parts[c]
        alm = mixed * beam_s[pl.ds(channel, 1), :]
        twisted = jnp.concatenate([-alm[3:4], alm[2:3], alm[1:2], -alm[0:1]], axis=0)
        alm_s[4 * k : 4 * k + 4, :width] = alm
        alm_s[4 * k : 4 * k + 4, width:] = twisted
    copies[1].wait()
    copies[2].wait()
    sums = lax.dot_general(alm_s[...].astype(BF16), leg_s[...], NN, preferred_element_type=F32)
    out[...] = sums.reshape(out.shape)


def lanes_of():
    lane = lax.broadcasted_iota(jnp.int32, (8, LANES), 1)
    return lane, lane % 2 == 1, lane % 4 < 2


def table_kernel(
    chan_of, mixing, orders, cycle_of, cycle_pixels, beam, legendre, noise,
    leg_out, mixed_out, pick_out, cos_out, sin_out, phase_out, weight_out,
    beam_s, noise_s, sems, *, chan, blk, slots
):
    width = leg_out.shape[1]
    first = chan() * width
    copies = [
        pltpu.make_async_copy(beam.at[:, pl.ds(first, width)], beam_s, sems.at[0]),
        pltpu.make_async_copy(noise, noise_s, sems.at[1]),
        pltpu.make_async_copy(legendre.at[0, 0, pl.ds(first, width), :], leg_out.at[0], sems.at[2]),
        pltpu.make_async_copy(legendre.at[1, 0, pl.ds(first, width), :], leg_out.at[1], sems.at[3]),
    ]
    for copy in copies:
        copy.start()
    count = orders.shape[0]
    lane, odd8, _ = lanes_of()
    order_row = jnp.zeros((8, LANES), F32)
    for i in range(count):
        order_row = jnp.where(lane // 4 == i, orders[i].astype(F32), order_row)
    m = order_row[:1]
    quarter = jnp.where(odd8[:1], 0.25, 0.0)
    start = blk() * slots
    cycles = [cycle_of[start + r] for r in range(slots)]
    row8 = lax.broadcasted_iota(jnp.int32, (8, LANES), 0)
    chosen8 = jnp.full((8, LANES), -1, jnp.int32)
    for r in range(slots):
        chosen8 = jnp.where(row8 == r, cycles[r], chosen8)
    pick_out[...] = jnp.where(lane == chosen8, 1.0, 0.0)
    half = noise.shape[0] // 2
    tall = half // slots
    steps_a = lax.broadcasted_iota(jnp.int32, (tall, LANES), 0).astype(F32) * m * 32.0
    steps_b = (2 * lax.broadcasted_iota(jnp.int32, (LANES, LANES), 0) + 1).astype(F32) * m
    pixel = (
        lax.broadcasted_iota(jnp.int32, (tall, LANES), 0) * LANES
        + lax.broadcasted_iota(jnp.int32, (tall, LANES), 1)
    )
    numbers = [cycle_pixels[cycles[r]] for r in range(slots)]
    for r in range(slots):
        number = jnp.full((1, LANES), numbers[r], jnp.int32).astype(F32)
        ya = turns_of(steps_a, number * 0.25)
        ya = ya - nearest(ya)
        cos_out[r] = cos_turns(ya)
        sin_out[r] = sin_turns(ya)
        yb = turns_of(steps_b, number * 2.0) - quarter
        yb = yb - nearest(yb)
        phase_out[r] = cos_turns(yb).astype(BF16)
    order = orders[blk()]
    degrees = first + lax.broadcasted_iota(jnp.int32, (1, width), 1)
    keep = jnp.where(degrees >= order, 1.0, 0.0)
    copies[0].wait()
    for k in range(chan_of.shape[0]):
        channel = chan_of[k]
        row = beam_s[pl.ds(channel, 1), :] * keep
        for c in range(mixed_out.shape[0]):
            mixed_out[c, 4 * k : 4 * k + 4, :] = jnp.broadcast_to(mixing[c, channel] * row, (4, width))
    copies[1].wait()
    for r in range(slots):
        inverse = 1.0 / jnp.full((1, LANES), numbers[r], jnp.int32).astype(F32)
        live = jnp.where(pixel < numbers[r], inverse, 0.0)
        weight_out[r, :tall] = noise_s[pl.ds(r, tall, stride=slots), :] * live
        weight_out[r, tall:] = noise_s[pl.ds(half + r, tall, stride=slots), :] * live
    copies[2].wait()
    copies[3].wait()


def cycle_kernel(coeffs, picked, cosines, sines, phases, weights, out):
    _, odd8, is_q8 = lanes_of()
    is_q = is_q8[:1]
    sign8 = jnp.where(odd8, -1.0, 1.0)
    row8 = lax.broadcasted_iota(jnp.int32, (8, LANES), 0)

    def swap(x):
        up = pltpu.roll(x, LANES - 1, 1)
        down = pltpu.roll(x, 1, 1)
        return jnp.where(odd8, down, up)

    slots, tall = cosines.shape[:2]
    pick = picked[...].astype(BF16)
    table = coeffs[...].reshape(LANES, LANES)
    x = lax.dot_general(pick, table, NT, preferred_element_type=F32)
    x_sign = x * sign8
    x_swap = swap(x)
    total_cos = jnp.zeros((8, LANES), F32)
    total_sin = jnp.zeros((8, LANES), F32)
    for r in range(slots):
        left = x_sign[r : r + 1] * cosines[r] - x_swap[r : r + 1] * sines[r]
        left = jnp.concatenate([jnp.where(is_q, left, 0.0), jnp.where(is_q, 0.0, left)], axis=0)
        maps = lax.dot_general(left.astype(BF16), phases[r], NT, preferred_element_type=F32)
        weighted = (weights[r] * maps).astype(BF16)
        back = lax.dot_general(weighted, phases[r], NN, preferred_element_type=F32)
        back = jnp.where(is_q, back[:tall], back[tall:])
        total_cos = jnp.where(row8 == r, jnp.sum(cosines[r] * back, axis=0, keepdims=True), total_cos)
        total_sin = jnp.where(row8 == r, jnp.sum(sines[r] * back, axis=0, keepdims=True), total_sin)
    grads = sign8 * total_cos - swap(total_sin)
    spread = lax.dot_general(grads.astype(BF16), pick, TN, preferred_element_type=F32)
    out[...] = spread.astype(BF16).reshape(out.shape)


def adjoint_kernel(grads, legendre, mixed, out):
    slots = grads.shape[0]
    straight = grads[...].astype(F32).reshape(slots * 4, LANES)
    row = lax.broadcasted_iota(jnp.int32, straight.shape, 0) % 4
    up = pltpu.roll(straight, straight.shape[0] - 1, 0)
    down = pltpu.roll(straight, 1, 0)
    up3 = pltpu.roll(straight, straight.shape[0] - 3, 0)
    down3 = pltpu.roll(straight, 3, 0)
    twisted = jnp.where(row == 0, -up3, jnp.where(row == 1, up, jnp.where(row == 2, down, -down3)))
    sums = lax.dot_general(straight.astype(BF16), legendre[0], NT, preferred_element_type=F32)
    sums = sums + lax.dot_general(twisted.astype(BF16), legendre[1], NT, preferred_element_type=F32)
    for c in range(out.shape[0]):
        pairs = jnp.sum((sums * mixed[c]).reshape(slots // 2, 8, sums.shape[1]), axis=0)
        out[c, :, 0, :] = pairs[:4] + pairs[4:]


def body(
    comp_alms,
    legendre,
    inv_noise,
    beam_window,
    mixing,
    channel_of,
    m_orders,
    cycle_of,
    cycle_pixels,
):
    slots = channel_of.shape[0]
    orders = m_orders.shape[0]
    cycles = legendre.shape[3]
    comps, _, _, width = comp_alms.shape
    where = dict(chan=lambda: lax.axis_index("chan"), blk=lambda: lax.axis_index("blk"))
    by_comp = mixing.T
    partial = pl.pallas_call(
        functools.partial(forward_kernel, **where),
        out_shape=pltpu.VMEM((slots, 4, cycles), F32),
        in_specs=[SMEM, SMEM, SMEM, ANY, ANY, ANY],
        out_specs=VMEM,
        scratch_shapes=[
            pltpu.VMEM(comp_alms.shape, F32),
            pltpu.VMEM((beam_window.shape[0], width), F32),
            pltpu.VMEM((2 * width, cycles), BF16),
            pltpu.VMEM((slots * 4, 2 * width), F32),
            pltpu.SemaphoreType.DMA((4,)),
        ],
        name="forward",
    )(channel_of, by_comp, m_orders, comp_alms, beam_window, legendre)
    pieces = move(partial, "chan")
    coeffs = jnp.sum(pieces, axis=0).astype(BF16)
    coeffs = move(jnp.broadcast_to(coeffs, (orders, 4, cycles)), "blk")
    held = inv_noise.shape[2]
    tall = inv_noise.shape[3] // LANES
    noise = inv_noise.reshape(2, held, tall, LANES).transpose(0, 2, 1, 3).reshape(2 * tall * held, LANES)
    legs, mixed, *tables = pl.pallas_call(
        functools.partial(table_kernel, slots=held, **where),
        out_shape=[
            pltpu.VMEM((2, width, cycles), BF16),
            pltpu.VMEM((comps, 4 * slots, width), F32),
            pltpu.VMEM((8, LANES), F32),
            pltpu.VMEM((held, tall, LANES), F32),
            pltpu.VMEM((held, tall, LANES), F32),
            pltpu.VMEM((held, LANES, LANES), BF16),
            pltpu.VMEM((held, 2 * tall, LANES), F32),
        ],
        in_specs=[SMEM, SMEM, SMEM, SMEM, SMEM, ANY, ANY, ANY],
        out_specs=[VMEM] * 7,
        scratch_shapes=[
            pltpu.VMEM((beam_window.shape[0], width), F32),
            pltpu.VMEM(noise.shape, F32),
            pltpu.SemaphoreType.DMA((4,)),
        ],
        name="tables",
    )(channel_of, by_comp, m_orders, cycle_of, cycle_pixels, beam_window, legendre, noise)
    grads = pl.pallas_call(
        cycle_kernel,
        out_shape=pltpu.VMEM((orders, 4, cycles), BF16),
        in_specs=[VMEM] * 6,
        out_specs=VMEM,
        name="cycles",
    )(in_vmem(coeffs), *map(in_vmem, tables))
    grads = jnp.sum(move(grads, "blk").astype(F32), axis=0).astype(BF16)
    grads = move(jnp.broadcast_to(grads, (slots, 4, cycles)), "chan")
    return pl.pallas_call(
        adjoint_kernel,
        out_shape=jax.ShapeDtypeStruct(comp_alms.shape, F32),
        in_specs=[VMEM] * 3,
        out_specs=VMEM,
        name="adjoint",
    )(in_vmem(grads), in_vmem(legs), in_vmem(mixed))


def solution(mesh):
    placed = (
        P(None, None, "blk", "chan"),
        P(None, "blk", None, None),
        P("chan", None, "blk", None),
        P(),
        P(),
        P(),
        P(),
        P(),
        P(),
    )
    return jax.shard_map(
        body, mesh=mesh, in_specs=placed, out_specs=P(None, None, "blk", "chan"), check_vma=False
    )
```

```python
import functools

import jax
import jax.numpy as jnp
from jax import lax
from jax.experimental import pallas as pl
from jax.experimental.pallas import tpu as pltpu
from jax.sharding import PartitionSpec as P

F32 = jnp.float32
BF16 = jnp.bfloat16
LANES = 128
NT = (((1,), (1,)), ((), ()))
NN = (((1,), (0,)), ((), ()))
COS = (0.9999999887921183, -19.739204415555925, 64.93911321613162, -85.45006149635309,
       60.16698573653733, -25.965151588112157, 6.525190124026944)
SIN = (6.28318530240345, -41.341700371179485, 81.60512965170976, -76.70298335354587,
       42.02566158843437, -14.898837201069828, 3.2367039052082127)

SMEM = pl.BlockSpec(memory_space=pltpu.SMEM)
VMEM = pl.BlockSpec(memory_space=pltpu.VMEM)
ANY = pl.BlockSpec(memory_space=pl.ANY)


def move(x, axis):
    return lax.all_to_all(x, axis, 0, 0, tiled=True)


def in_vmem(x):
    return pltpu.with_memory_space_constraint(x, pltpu.VMEM)


def nearest(x):
    return jnp.floor(x + 0.5)


def poly(z, terms):
    total = jnp.full_like(z, terms[-1])
    for term in terms[-2::-1]:
        total = total * z + term
    return total


def cos_turns(y):
    return poly(y * y, COS)


def sin_turns(y):
    return y * poly(y * y, SIN)


def turns_of(steps, period):
    inverse = 1.0 / period
    rest = steps - nearest(steps * inverse) * period
    return rest * inverse


def forward_kernel(
    chan_of, mixing, orders, comp, beam, legendre, out, leg, mixed_out, comp_s, beam_s, alm_s, sems, *, chan, blk
):
    width = comp.shape[3]
    first = chan() * width
    copies = [
        pltpu.make_async_copy(beam.at[:, pl.ds(first, width)], beam_s, sems.at[0]),
        pltpu.make_async_copy(legendre.at[0, 0, pl.ds(first, width), :], leg.at[pl.ds(0, width)], sems.at[1]),
        pltpu.make_async_copy(legendre.at[1, 0, pl.ds(first, width), :], leg.at[pl.ds(width, width)], sems.at[2]),
        pltpu.make_async_copy(comp, comp_s, sems.at[3]),
    ]
    for copy in copies:
        copy.start()
    order = orders[blk()]
    degrees = first + lax.broadcasted_iota(jnp.int32, (1, width), 1)
    keep = jnp.where(degrees >= order, 1.0, 0.0)
    copies[3].wait()
    parts = [comp_s[c, :, 0, :] for c in range(comp.shape[0])]
    copies[0].wait()
    for k in range(out.shape[0]):
        channel = chan_of[k]
        row = beam_s[pl.ds(channel, 1), :] * keep
        mixed = mixing[0, channel] * parts[0]
        for c in range(1, len(parts)):
            mixed = mixed + mixing[c, channel] * parts[c]
        alm = mixed * row
        twisted = jnp.concatenate([-alm[3:4], alm[2:3], alm[1:2], -alm[0:1]], axis=0)
        alm_s[4 * k : 4 * k + 4, :width] = alm
        alm_s[4 * k : 4 * k + 4, width:] = twisted
        for c in range(len(parts)):
            mixed_out[c, 4 * k : 4 * k + 4, :] = jnp.broadcast_to(mixing[c, channel] * row, (4, width))
    copies[1].wait()
    copies[2].wait()
    sums = lax.dot_general(alm_s[...].astype(BF16), leg[...], NN, preferred_element_type=F32)
    out[...] = sums.reshape(out.shape)


def cycle_matrix_kernel(
    orders, cycle_of, cycle_pixels, cycle_row, noise, out, pick_out, noise_s, weight_s, order_s, sems, *, blk, slots
):
    copy = pltpu.make_async_copy(noise, noise_s, sems.at[0])
    copy.start()
    count = orders.shape[0]
    start = blk() * slots
    numbers = [cycle_pixels[cycle_of[start + r]] for r in range(slots)]
    for i in range(count):
        order_s[i : i + 1, :] = jnp.full((1, LANES), orders[i], jnp.int32).astype(F32)
    m = order_s[...]
    square = (LANES, LANES)
    slot_of = lax.broadcasted_iota(jnp.int32, (2 * LANES, LANES), 0)
    slot_of = 4 * (slot_of // 8) + slot_of % 4
    expand = jnp.where(slot_of == lax.broadcasted_iota(jnp.int32, slot_of.shape, 1), 1.0, 0.0).astype(BF16)
    at_cycle = jnp.where(lax.broadcasted_iota(jnp.int32, square, 0) == cycle_row[...], 1.0, 0.0).astype(BF16)
    pick_out[...] = lax.dot_general(expand, at_cycle, NT, preferred_element_type=F32).astype(BF16)

    half = noise.shape[0] // 2
    tall = half // slots
    pixel = (
        lax.broadcasted_iota(jnp.int32, (tall, LANES), 0) * LANES
        + lax.broadcasted_iota(jnp.int32, (tall, LANES), 1)
    )
    copy.wait()
    for r in range(slots):
        inverse = 1.0 / jnp.full((1, LANES), numbers[r], jnp.int32).astype(F32)
        live = jnp.where(pixel < numbers[r], inverse, 0.0)
        weight_s[r, 0] = noise_s[pl.ds(r, tall, stride=slots), :] * live
        weight_s[r, 1] = noise_s[pl.ds(half + r, tall, stride=slots), :] * live

    source = lax.broadcasted_iota(jnp.int32, (2 * LANES, 1), 0)
    x, t, xx, ii = source // 128, source // 64 % 2, source // 32 % 2, source % 32
    target = (ii // 16) * 128 + (ii % 16) * 8 + x * 4 + t * 2 + xx
    value = jnp.where(x == xx, 1.0, -1.0)
    order_lanes = jnp.where(
        lax.broadcasted_iota(jnp.int32, (2 * LANES, 2 * LANES), 1) == target, value, 0.0
    ).astype(BF16)

    odd_steps = (2 * lax.broadcasted_iota(jnp.int32, (count, LANES), 1) + 1).astype(F32) * m
    unroll = 8
    for r in range(slots):
        number = jnp.full((1, LANES), numbers[r], jnp.int32).astype(F32)
        turn = turns_of(m * 32.0, number * 0.25)
        turn = turn - nearest(turn)
        turn_cos, turn_sin = cos_turns(turn), sin_turns(turn)
        base = turns_of(odd_steps, number * 2.0)
        base = base - nearest(base)

        def add_pixels(chunk, state, r=r, turn_cos=turn_cos, turn_sin=turn_sin):
            total, c, s = state
            first = pl.multiple_of(chunk * unroll, unroll)
            rows_q = weight_s[r, 0, pl.ds(first, unroll), :]
            rows_u = weight_s[r, 1, pl.ds(first, unroll), :]
            for pair in range(unroll // 2):
                phases, weighted = [], []
                for step in (2 * pair, 2 * pair + 1):
                    q, u = rows_q[step : step + 1], rows_u[step : step + 1]
                    phases.append(jnp.concatenate([c, s], axis=0).astype(BF16))
                    weighted.append(jnp.concatenate([q * c, q * s, u * c, u * s], axis=0).astype(BF16))
                    c, s = c * turn_cos - s * turn_sin, s * turn_cos + c * turn_sin
                total = total + lax.dot_general(
                    jnp.concatenate(phases, axis=1),
                    jnp.concatenate(weighted, axis=1),
                    NT,
                    preferred_element_type=F32,
                )
            return total, c, s

        total, _, _ = lax.fori_loop(
            0,
            tall // unroll,
            add_pixels,
            (jnp.zeros((2 * count, LANES), F32), cos_turns(base), sin_turns(base)),
        )
        pair = jnp.concatenate([total[:count], total[count:]], axis=1).astype(BF16)
        placed = lax.dot_general(pair, order_lanes, NN, preferred_element_type=F32)
        out[:, r, :] = placed[:, :LANES]
        out[:, slots + r, :] = placed[:, LANES:]


def join_kernel(pieces, matrix, out):
    coeffs = jnp.sum(pieces[...], axis=0)
    twice = jnp.concatenate([coeffs, coeffs], axis=0)
    for i in range(out.shape[0]):
        out[i] = jnp.concatenate([matrix[i], twice], axis=0).astype(BF16)


def cycle_kernel(received, pick, out):
    values = received[...].astype(F32)
    matrix = values[:, :8, :].reshape(2 * LANES, LANES)
    coeffs = values[:, 8:, :].reshape(2 * LANES, LANES).astype(BF16)
    picks = pick[...]
    low = lax.dot_general(picks, coeffs[:LANES], NT, preferred_element_type=F32)
    high = lax.dot_general(picks, coeffs[LANES:], NT, preferred_element_type=F32)
    upper = lax.broadcasted_iota(jnp.int32, low.shape, 0) % 8 >= 4
    product = matrix * jnp.where(upper, high, low)
    lane = lax.broadcasted_iota(jnp.int32, (8, LANES), 1)
    part = lane // 2 % 2 * 2 + lane // 4 % 2
    gather = jnp.where(part == lax.broadcasted_iota(jnp.int32, part.shape, 0), 1.0, 0.0).astype(BF16)

    def exact(dot, x):
        head = x.astype(BF16)
        return dot(head) + dot((x - head.astype(F32)).astype(BF16))

    by_slot = exact(lambda y: lax.dot_general(gather, y, NT, preferred_element_type=F32), product)
    grads = exact(lambda y: lax.dot_general(y, picks, NN, preferred_element_type=F32), by_slot)
    out[...] = jnp.broadcast_to(grads[:4].astype(BF16)[None], out.shape)


def adjoint_kernel(grads, legendre, mixed, out):
    slots = grads.shape[0]
    width = out.shape[3]
    straight = grads[...].astype(F32).reshape(slots * 4, LANES)
    row = lax.broadcasted_iota(jnp.int32, straight.shape, 0) % 4
    up = pltpu.roll(straight, straight.shape[0] - 1, 0)
    down = pltpu.roll(straight, 1, 0)
    up3 = pltpu.roll(straight, straight.shape[0] - 3, 0)
    down3 = pltpu.roll(straight, 3, 0)
    twisted = jnp.where(row == 0, -up3, jnp.where(row == 1, up, jnp.where(row == 2, down, -down3)))
    sums = lax.dot_general(straight.astype(BF16), legendre[:width], NT, preferred_element_type=F32)
    sums = sums + lax.dot_general(twisted.astype(BF16), legendre[width:], NT, preferred_element_type=F32)
    for c in range(out.shape[0]):
        pairs = jnp.sum((sums * mixed[c]).reshape(slots // 2, 8, sums.shape[1]), axis=0)
        out[c, :, 0, :] = pairs[:4] + pairs[4:]


def body(
    comp_alms,
    legendre,
    inv_noise,
    beam_window,
    mixing,
    channel_of,
    m_orders,
    cycle_of,
    cycle_pixels,
):
    slots = channel_of.shape[0]
    orders = m_orders.shape[0]
    cycles = legendre.shape[3]
    comps, _, _, width = comp_alms.shape
    chan = functools.partial(lax.axis_index, "chan")
    blk = functools.partial(lax.axis_index, "blk")
    partial, legs, mixed = pl.pallas_call(
        functools.partial(forward_kernel, chan=chan, blk=blk),
        out_shape=[
            jax.ShapeDtypeStruct((slots, 4, cycles), F32),
            pltpu.VMEM((2 * width, cycles), BF16),
            pltpu.VMEM((comps, 4 * slots, width), F32),
        ],
        in_specs=[SMEM, SMEM, SMEM, ANY, ANY, ANY],
        out_specs=[VMEM] * 3,
        scratch_shapes=[
            pltpu.VMEM(comp_alms.shape, F32),
            pltpu.VMEM((beam_window.shape[0], width), F32),
            pltpu.VMEM((slots * 4, 2 * width), F32),
            pltpu.SemaphoreType.DMA((4,)),
        ],
        name="forward",
    )(channel_of, mixing.T, m_orders, comp_alms, beam_window, legendre)
    pieces = move(partial, "chan")
    held = inv_noise.shape[2]
    tall = inv_noise.shape[3] // LANES
    noise = inv_noise.reshape(2, held, tall, LANES).transpose(0, 2, 1, 3).reshape(2 * tall * held, LANES)
    matrix, pick = pl.pallas_call(
        functools.partial(cycle_matrix_kernel, blk=blk, slots=held),
        out_shape=[pltpu.VMEM((orders, 2 * held, LANES), F32), pltpu.VMEM((2 * LANES, LANES), BF16)],
        in_specs=[SMEM, SMEM, SMEM, VMEM, ANY],
        out_specs=[VMEM] * 2,
        scratch_shapes=[
            pltpu.VMEM(noise.shape, F32),
            pltpu.VMEM((held, 2, tall, LANES), F32),
            pltpu.VMEM((orders, LANES), F32),
            pltpu.SemaphoreType.DMA((1,)),
        ],
        name="matrices",
    )(m_orders, cycle_of, cycle_pixels, cycle_of.reshape(1, -1), noise)
    message = pl.pallas_call(
        join_kernel,
        out_shape=pltpu.VMEM((orders, 16, LANES), BF16),
        in_specs=[VMEM] * 2,
        out_specs=VMEM,
        name="join",
    )(in_vmem(pieces), in_vmem(matrix))
    grads = pl.pallas_call(
        cycle_kernel,
        out_shape=pltpu.VMEM((slots, 4, cycles), BF16),
        in_specs=[VMEM] * 2,
        out_specs=VMEM,
        name="cycles",
    )(in_vmem(move(message, "blk")), in_vmem(pick))
    return pl.pallas_call(
        adjoint_kernel,
        out_shape=jax.ShapeDtypeStruct(comp_alms.shape, F32),
        in_specs=[VMEM] * 3,
        out_specs=VMEM,
        name="adjoint",
    )(in_vmem(move(grads, "chan")), in_vmem(legs), in_vmem(mixed))


def solution(mesh):
    placed = (
        P(None, None, "blk", "chan"),
        P(None, "blk", None, None),
        P("chan", None, "blk", None),
        P(),
        P(),
        P(),
        P(),
        P(),
        P(),
    )
    return jax.shard_map(
        body, mesh=mesh, in_specs=placed, out_specs=P(None, None, "blk", "chan"), check_vma=False
    )
```

```python
import functools

import jax
import jax.numpy as jnp
from jax import lax
from jax.experimental import pallas as pl
from jax.experimental.pallas import tpu as pltpu
from jax.sharding import PartitionSpec as P

F32 = jnp.float32
BF16 = jnp.bfloat16
LANES = 128
NT = (((1,), (1,)), ((), ()))
NN = (((1,), (0,)), ((), ()))
COS = (0.9999999887921183, -19.739204415555925, 64.93911321613162, -85.45006149635309,
       60.16698573653733, -25.965151588112157, 6.525190124026944)
SIN = (6.28318530240345, -41.341700371179485, 81.60512965170976, -76.70298335354587,
       42.02566158843437, -14.898837201069828, 3.2367039052082127)

VMEM = pl.BlockSpec(memory_space=pltpu.VMEM)
ANY = pl.BlockSpec(memory_space=pl.ANY)


def move(x, axis):
    return lax.all_to_all(x, axis, 0, 0, tiled=True)


def in_vmem(x):
    return pltpu.with_memory_space_constraint(x, pltpu.VMEM)


def nearest(x):
    return jnp.floor(x + 0.5)


def poly(z, terms):
    total = jnp.full_like(z, terms[-1])
    for term in terms[-2::-1]:
        total = total * z + term
    return total


def cos_turns(y):
    return poly(y * y, COS)


def sin_turns(y):
    return y * poly(y * y, SIN)


def turns_of(steps, period):
    inverse = 1.0 / period
    rest = steps - nearest(steps * inverse) * period
    return rest * inverse


def forward_kernel(
    chan_of_hbm, mixing_hbm, orders_hbm, comp, beam, legendre, out, leg, mixed_out,
    chan_of, mixing, orders, comp_s, beam_s, alm_s, sems, *, chan, blk
):
    width = comp.shape[3]
    first = chan() * width
    copies = [
        pltpu.make_async_copy(beam.at[:, pl.ds(first, width)], beam_s, sems.at[0]),
        pltpu.make_async_copy(legendre.at[0, 0, pl.ds(first, width), :], leg.at[pl.ds(0, width)], sems.at[1]),
        pltpu.make_async_copy(legendre.at[1, 0, pl.ds(first, width), :], leg.at[pl.ds(width, width)], sems.at[2]),
        pltpu.make_async_copy(comp, comp_s, sems.at[3]),
        pltpu.make_async_copy(chan_of_hbm, chan_of, sems.at[4]),
        pltpu.make_async_copy(mixing_hbm, mixing, sems.at[5]),
        pltpu.make_async_copy(orders_hbm, orders, sems.at[6]),
    ]
    for copy in copies[::-1]:
        copy.start()
    degrees = first + lax.broadcasted_iota(jnp.int32, (1, width), 1)
    for copy in (copies[0], *copies[3:]):
        copy.wait()
    order = orders[blk()]
    keep = jnp.where(degrees >= order, 1.0, 0.0)
    parts = [comp_s[c, :, 0, :] for c in range(comp.shape[0])]
    for k in range(out.shape[0]):
        channel = chan_of[k]
        row = beam_s[pl.ds(channel, 1), :] * keep
        mixed = mixing[0, channel] * parts[0]
        for c in range(1, len(parts)):
            mixed = mixed + mixing[c, channel] * parts[c]
        alm = mixed * row
        twisted = jnp.concatenate([-alm[3:4], alm[2:3], alm[1:2], -alm[0:1]], axis=0)
        alm_s[4 * k : 4 * k + 4, :width] = alm
        alm_s[4 * k : 4 * k + 4, width:] = twisted
        for c in range(len(parts)):
            mixed_out[c, 4 * k : 4 * k + 4, :] = jnp.broadcast_to(mixing[c, channel] * row, (4, width))
    copies[1].wait()
    copies[2].wait()
    sums = lax.dot_general(alm_s[...].astype(BF16), leg[...], NN, preferred_element_type=F32)
    out[...] = sums.reshape(out.shape)


def cycle_matrix_kernel(
    orders_hbm, cycle_of_hbm, cycle_pixels_hbm, cycle_row_hbm, noise, out, pick_out,
    orders, cycle_of, cycle_pixels, cycle_row, noise_s, weight_s, order_s, sems, *, blk, slots
):
    pairs = (
        (orders_hbm, orders),
        (cycle_of_hbm, cycle_of),
        (cycle_pixels_hbm, cycle_pixels),
        (cycle_row_hbm, cycle_row),
        (noise, noise_s),
    )
    copies = [pltpu.make_async_copy(src, dst, sems.at[n]) for n, (src, dst) in enumerate(pairs)]
    for copy in copies:
        copy.start()
    count = orders.shape[0]
    start = blk() * slots
    slot_of = lax.broadcasted_iota(jnp.int32, (2 * LANES, LANES), 0)
    slot_of = 4 * (slot_of // 8) + slot_of % 4
    expand = jnp.where(slot_of == lax.broadcasted_iota(jnp.int32, slot_of.shape, 1), 1.0, 0.0).astype(BF16)
    source = lax.broadcasted_iota(jnp.int32, (2 * LANES, 1), 0)
    x, t, xx, ii = source // 128, source // 64 % 2, source // 32 % 2, source % 32
    target = (ii // 16) * 128 + (ii % 16) * 8 + x * 4 + t * 2 + xx
    value = jnp.where(x == xx, 1.0, -1.0)
    order_lanes = jnp.where(
        lax.broadcasted_iota(jnp.int32, (2 * LANES, 2 * LANES), 1) == target, value, 0.0
    ).astype(BF16)
    for copy in copies[:4]:
        copy.wait()
    numbers = [cycle_pixels[cycle_of[start + r]] for r in range(slots)]
    for i in range(count):
        order_s[i : i + 1, :] = jnp.full((1, LANES), orders[i], jnp.int32).astype(F32)
    m = order_s[...]
    at_cycle = jnp.where(
        lax.broadcasted_iota(jnp.int32, (LANES, LANES), 0) == cycle_row[...], 1.0, 0.0
    ).astype(BF16)
    pick_out[...] = lax.dot_general(expand, at_cycle, NT, preferred_element_type=F32).astype(BF16)
    odd_steps = (2 * lax.broadcasted_iota(jnp.int32, (count, LANES), 1) + 1).astype(F32) * m
    turns, states = [], []
    for r in range(slots):
        number = jnp.full((1, LANES), numbers[r], jnp.int32).astype(F32)
        turn = turns_of(m * 32.0, number * 0.25)
        turn = turn - nearest(turn)
        turns.append((cos_turns(turn), sin_turns(turn)))
        base = turns_of(odd_steps, number * 2.0)
        base = base - nearest(base)
        states.append((jnp.zeros((4 * count, 2 * count), F32), cos_turns(base), sin_turns(base)))

    half = noise.shape[0] // 2
    tall = half // slots
    pixel = (
        lax.broadcasted_iota(jnp.int32, (tall, LANES), 0) * LANES
        + lax.broadcasted_iota(jnp.int32, (tall, LANES), 1)
    )
    copies[4].wait()
    for r in range(slots):
        inverse = 1.0 / jnp.full((1, LANES), numbers[r], jnp.int32).astype(F32)
        live = jnp.where(pixel < numbers[r], inverse, 0.0)
        weight_s[r, 0] = noise_s[pl.ds(r, tall, stride=slots), :] * live
        weight_s[r, 1] = noise_s[pl.ds(half + r, tall, stride=slots), :] * live

    unroll = 16

    def add_pixels(chunk, states):
        first = pl.multiple_of(chunk * unroll, unroll)
        rows = [[weight_s[r, t, pl.ds(first, unroll), :] for t in (0, 1)] for r in range(slots)]
        states = list(states)
        for even in range(0, unroll, 2):
            for r in range(slots):
                total, c, s = states[r]
                turn_cos, turn_sin = turns[r]
                phases, weighted = [], []
                for step in (even, even + 1):
                    q, u = (rows[r][t][step : step + 1] for t in (0, 1))
                    phases.append(jnp.concatenate([c, s], axis=0).astype(BF16))
                    weighted.append(jnp.concatenate([q * c, q * s, u * c, u * s], axis=0).astype(BF16))
                    c, s = c * turn_cos - s * turn_sin, s * turn_cos + c * turn_sin
                total = total + lax.dot_general(
                    jnp.concatenate(weighted, axis=1),
                    jnp.concatenate(phases, axis=1),
                    NT,
                    preferred_element_type=F32,
                )
                states[r] = (total, c, s)
        return tuple(states)

    states = lax.fori_loop(0, tall // unroll, add_pixels, tuple(states))
    for r in range(slots):
        total = states[r][0]
        rows = [total[(2 * t + x) * count : (2 * t + x + 1) * count] for x in (0, 1) for t in (0, 1)]
        placed = lax.dot_general(
            jnp.concatenate(rows, axis=1).astype(BF16), order_lanes, NN, preferred_element_type=F32
        )
        out[:, r, :] = placed[:, :LANES]
        out[:, slots + r, :] = placed[:, LANES:]


def join_kernel(pieces, matrix, out):
    coeffs = jnp.sum(pieces[...], axis=0)
    twice = jnp.concatenate([coeffs, coeffs], axis=0)
    for i in range(out.shape[0]):
        out[i] = jnp.concatenate([matrix[i], twice], axis=0).astype(BF16)


def cycle_kernel(received, pick, out):
    values = received[...].astype(F32)
    matrix = values[:, :8, :].reshape(2 * LANES, LANES)
    coeffs = values[:, 8:, :].reshape(2 * LANES, LANES).astype(BF16)
    picks = pick[...]
    low = lax.dot_general(picks, coeffs[:LANES], NT, preferred_element_type=F32)
    high = lax.dot_general(picks, coeffs[LANES:], NT, preferred_element_type=F32)
    upper = lax.broadcasted_iota(jnp.int32, low.shape, 0) % 8 >= 4
    product = matrix * jnp.where(upper, high, low)
    lane = lax.broadcasted_iota(jnp.int32, (8, LANES), 1)
    part = lane // 2 % 2 * 2 + lane // 4 % 2
    gather = jnp.where(part == lax.broadcasted_iota(jnp.int32, part.shape, 0), 1.0, 0.0).astype(BF16)

    def exact(dot, x):
        head = x.astype(BF16)
        return dot(head) + dot((x - head.astype(F32)).astype(BF16))

    by_slot = exact(lambda y: lax.dot_general(gather, y, NT, preferred_element_type=F32), product)
    grads = exact(lambda y: lax.dot_general(y, picks, NN, preferred_element_type=F32), by_slot)
    out[...] = jnp.broadcast_to(grads[:4].astype(BF16)[None], out.shape)


def adjoint_kernel(grads, legendre, mixed, out):
    slots = grads.shape[0]
    width = out.shape[3]
    straight = grads[...].astype(F32).reshape(slots * 4, LANES)
    row = lax.broadcasted_iota(jnp.int32, straight.shape, 0) % 4
    up = pltpu.roll(straight, straight.shape[0] - 1, 0)
    down = pltpu.roll(straight, 1, 0)
    up3 = pltpu.roll(straight, straight.shape[0] - 3, 0)
    down3 = pltpu.roll(straight, 3, 0)
    twisted = jnp.where(row == 0, -up3, jnp.where(row == 1, up, jnp.where(row == 2, down, -down3)))
    sums = lax.dot_general(straight.astype(BF16), legendre[:width], NT, preferred_element_type=F32)
    sums = sums + lax.dot_general(twisted.astype(BF16), legendre[width:], NT, preferred_element_type=F32)
    for c in range(out.shape[0]):
        pairs = jnp.sum((sums * mixed[c]).reshape(slots // 2, 8, sums.shape[1]), axis=0)
        out[c, :, 0, :] = pairs[:4] + pairs[4:]


def body(
    comp_alms,
    legendre,
    inv_noise,
    beam_window,
    mixing,
    channel_of,
    m_orders,
    cycle_of,
    cycle_pixels,
):
    slots = channel_of.shape[0]
    orders = m_orders.shape[0]
    cycles = legendre.shape[3]
    comps, _, _, width = comp_alms.shape
    chan = functools.partial(lax.axis_index, "chan")
    blk = functools.partial(lax.axis_index, "blk")
    partial, legs, mixed = pl.pallas_call(
        functools.partial(forward_kernel, chan=chan, blk=blk),
        out_shape=[
            jax.ShapeDtypeStruct((slots, 4, cycles), F32),
            pltpu.VMEM((2 * width, cycles), BF16),
            pltpu.VMEM((comps, 4 * slots, width), F32),
        ],
        in_specs=[ANY] * 6,
        out_specs=[VMEM] * 3,
        scratch_shapes=[
            pltpu.SMEM(channel_of.shape, jnp.int32),
            pltpu.SMEM(mixing.shape[::-1], F32),
            pltpu.SMEM(m_orders.shape, jnp.int32),
            pltpu.VMEM(comp_alms.shape, F32),
            pltpu.VMEM((beam_window.shape[0], width), F32),
            pltpu.VMEM((slots * 4, 2 * width), F32),
            pltpu.SemaphoreType.DMA((7,)),
        ],
        name="forward",
    )(channel_of, mixing.T, m_orders, comp_alms, beam_window, legendre)
    pieces = move(partial, "chan")
    held = inv_noise.shape[2]
    tall = inv_noise.shape[3] // LANES
    noise = inv_noise.reshape(2, held, tall, LANES).transpose(0, 2, 1, 3).reshape(2 * tall * held, LANES)
    matrix, pick = pl.pallas_call(
        functools.partial(cycle_matrix_kernel, blk=blk, slots=held),
        out_shape=[pltpu.VMEM((orders, 2 * held, LANES), F32), pltpu.VMEM((2 * LANES, LANES), BF16)],
        in_specs=[ANY] * 5,
        out_specs=[VMEM] * 2,
        scratch_shapes=[
            pltpu.SMEM(m_orders.shape, jnp.int32),
            pltpu.SMEM(cycle_of.shape, jnp.int32),
            pltpu.SMEM(cycle_pixels.shape, jnp.int32),
            pltpu.VMEM((1, cycles), jnp.int32),
            pltpu.VMEM(noise.shape, F32),
            pltpu.VMEM((held, 2, tall, LANES), F32),
            pltpu.VMEM((orders, LANES), F32),
            pltpu.SemaphoreType.DMA((5,)),
        ],
        name="matrices",
    )(m_orders, cycle_of, cycle_pixels, cycle_of.reshape(1, -1), noise)
    message = pl.pallas_call(
        join_kernel,
        out_shape=pltpu.VMEM((orders, 16, LANES), BF16),
        in_specs=[VMEM] * 2,
        out_specs=VMEM,
        name="join",
    )(in_vmem(pieces), in_vmem(matrix))
    grads = pl.pallas_call(
        cycle_kernel,
        out_shape=pltpu.VMEM((slots, 4, cycles), BF16),
        in_specs=[VMEM] * 2,
        out_specs=VMEM,
        name="cycles",
    )(in_vmem(move(message, "blk")), in_vmem(pick))
    return pl.pallas_call(
        adjoint_kernel,
        out_shape=jax.ShapeDtypeStruct(comp_alms.shape, F32),
        in_specs=[VMEM] * 3,
        out_specs=VMEM,
        name="adjoint",
    )(in_vmem(move(grads, "chan")), in_vmem(legs), in_vmem(mixed))


def solution(mesh):
    placed = (
        P(None, None, "blk", "chan"),
        P(None, "blk", None, None),
        P("chan", None, "blk", None),
        P(),
        P(),
        P(),
        P(),
        P(),
        P(),
    )
    return jax.shard_map(
        body, mesh=mesh, in_specs=placed, out_specs=P(None, None, "blk", "chan"), check_vma=False
    )
```

```python
import functools

import jax
import jax.numpy as jnp
from jax import lax
from jax.experimental import pallas as pl
from jax.experimental.pallas import tpu as pltpu
from jax.sharding import PartitionSpec as P

F32 = jnp.float32
BF16 = jnp.bfloat16
LANES = 128
NT = (((1,), (1,)), ((), ()))
NN = (((1,), (0,)), ((), ()))
COS = (0.9999999887921183, -19.739204415555925, 64.93911321613162, -85.45006149635309,
       60.16698573653733, -25.965151588112157, 6.525190124026944)
SIN = (6.28318530240345, -41.341700371179485, 81.60512965170976, -76.70298335354587,
       42.02566158843437, -14.898837201069828, 3.2367039052082127)

VMEM = pl.BlockSpec(memory_space=pltpu.VMEM)
ANY = pl.BlockSpec(memory_space=pl.ANY)


def move(x, axis):
    return lax.all_to_all(x, axis, 0, 0, tiled=True)


def in_vmem(x):
    return pltpu.with_memory_space_constraint(x, pltpu.VMEM)


def nearest(x):
    return jnp.floor(x + 0.5)


def poly(z, terms):
    total = jnp.full_like(z, terms[-1])
    for term in terms[-2::-1]:
        total = total * z + term
    return total


def cos_turns(y):
    return poly(y * y, COS)


def sin_turns(y):
    return y * poly(y * y, SIN)


def turns_of(steps, period):
    inverse = 1.0 / period
    rest = steps - nearest(steps * inverse) * period
    return rest * inverse


def forward_kernel(
    chan_of_hbm, mixing_hbm, orders_hbm, cycle_of_hbm, cycle_pixels_hbm, cycle_row_hbm, comp, beam, legendre, noise,
    out, leg, mixed_out, noise_out, order_out, number_out, cycle_row_out,
    chan_of, mixing, orders, cycle_of, cycle_pixels, comp_s, beam_s, alm_s, sems, *, chan, blk, slots
):
    width = comp.shape[3]
    first = chan() * width
    copies = [
        pltpu.make_async_copy(beam.at[:, pl.ds(first, width)], beam_s, sems.at[0]),
        pltpu.make_async_copy(legendre.at[0, 0, pl.ds(first, width), :], leg.at[pl.ds(0, width)], sems.at[1]),
        pltpu.make_async_copy(legendre.at[1, 0, pl.ds(first, width), :], leg.at[pl.ds(width, width)], sems.at[2]),
        pltpu.make_async_copy(comp, comp_s, sems.at[3]),
        pltpu.make_async_copy(chan_of_hbm, chan_of, sems.at[4]),
        pltpu.make_async_copy(mixing_hbm, mixing, sems.at[5]),
        pltpu.make_async_copy(orders_hbm, orders, sems.at[6]),
        pltpu.make_async_copy(cycle_of_hbm, cycle_of, sems.at[7]),
        pltpu.make_async_copy(cycle_pixels_hbm, cycle_pixels, sems.at[8]),
        pltpu.make_async_copy(cycle_row_hbm, cycle_row_out, sems.at[9]),
        pltpu.make_async_copy(noise, noise_out, sems.at[10]),
    ]
    for n in (4, 5, 6, 3, 0, 1, 2, 7, 8, 9, 10):
        copies[n].start()
    degrees = first + lax.broadcasted_iota(jnp.int32, (1, width), 1)
    for n in (4, 5, 6, 3, 0):
        copies[n].wait()
    order = orders[blk()]
    keep = jnp.where(degrees >= order, 1.0, 0.0)
    parts = [comp_s[c, :, 0, :] for c in range(comp.shape[0])]
    for k in range(out.shape[0]):
        channel = chan_of[k]
        row = beam_s[pl.ds(channel, 1), :] * keep
        mixed = mixing[0, channel] * parts[0]
        for c in range(1, len(parts)):
            mixed = mixed + mixing[c, channel] * parts[c]
        alm = mixed * row
        twisted = jnp.concatenate([-alm[3:4], alm[2:3], alm[1:2], -alm[0:1]], axis=0)
        alm_s[4 * k : 4 * k + 4, :width] = alm
        alm_s[4 * k : 4 * k + 4, width:] = twisted
        for c in range(len(parts)):
            mixed_out[c, 4 * k : 4 * k + 4, :] = jnp.broadcast_to(mixing[c, channel] * row, (4, width))
    copies[1].wait()
    copies[2].wait()
    sums = lax.dot_general(alm_s[...].astype(BF16), leg[...], NN, preferred_element_type=F32)
    out[...] = sums.reshape(out.shape)
    for i in range(orders.shape[0]):
        order_out[i : i + 1, :] = jnp.full((1, LANES), orders[i], jnp.int32).astype(F32)
    for copy in copies[7:]:
        copy.wait()
    start = blk() * slots
    for r in range(slots):
        number_out[r : r + 1, :] = jnp.full((1, LANES), cycle_pixels[cycle_of[start + r]], jnp.int32).astype(F32)


def cycle_matrix_kernel(order_rows, numbers, cycle_row, noise, out, pick_out, weight_s):
    count = order_rows.shape[0]
    slots = out.shape[1]
    square = (LANES, LANES)
    row = lax.broadcasted_iota(jnp.int32, square, 0)
    same = jnp.where(row == lax.broadcasted_iota(jnp.int32, square, 1), 1.0, 0.0).astype(BF16)
    at_cycle = jnp.where(row == cycle_row[...], 1.0, 0.0).astype(BF16)
    pick_out[...] = lax.dot_general(same, at_cycle, NT, preferred_element_type=F32).astype(BF16)
    m = order_rows[...]
    odd_steps = (2 * lax.broadcasted_iota(jnp.int32, (count, LANES), 1) + 1).astype(F32) * m
    half = noise.shape[0] // 2
    tall = half // slots
    pixel = (
        lax.broadcasted_iota(jnp.int32, (tall, LANES), 0) * LANES
        + lax.broadcasted_iota(jnp.int32, (tall, LANES), 1)
    ).astype(F32)
    turns, states = [], []
    for r in range(slots):
        number = numbers[r : r + 1, :]
        live = jnp.where(pixel < number, 1.0 / number, 0.0)
        weight_s[r, 0] = noise[pl.ds(r, tall, stride=slots), :] * live
        weight_s[r, 1] = noise[pl.ds(half + r, tall, stride=slots), :] * live
        turn = turns_of(m * 32.0, number * 0.25)
        turn = turn - nearest(turn)
        turns.append((cos_turns(turn), sin_turns(turn)))
        base = turns_of(odd_steps, number * 2.0)
        base = base - nearest(base)
        states.append((jnp.zeros((4 * count, 2 * count), F32), cos_turns(base), sin_turns(base)))

    for even in range(0, tall, 2):
        for r in range(slots):
            total, c, s = states[r]
            turn_cos, turn_sin = turns[r]
            phases, weighted = [], []
            for step in (even, even + 1):
                q, u = (weight_s[r, t, step : step + 1, :] for t in (0, 1))
                phases.append(jnp.concatenate([c, s], axis=0).astype(BF16))
                weighted.append(jnp.concatenate([q * c, q * s, u * c, u * s], axis=0).astype(BF16))
                c, s = c * turn_cos - s * turn_sin, s * turn_cos + c * turn_sin
            total = total + lax.dot_general(
                jnp.concatenate(weighted, axis=1),
                jnp.concatenate(phases, axis=1),
                NT,
                preferred_element_type=F32,
            )
            states[r] = (total, c, s)

    source = lax.broadcasted_iota(jnp.int32, (2 * LANES, 1), 0)
    x, t, xx, ii = source // 128, source // 64 % 2, source // 32 % 2, source % 32
    target = (ii // 16) * 128 + (ii % 16) * 8 + x * 4 + t * 2 + xx
    value = jnp.where(x == xx, 1.0, -1.0)
    order_lanes = jnp.where(
        lax.broadcasted_iota(jnp.int32, (2 * LANES, 2 * LANES), 1) == target, value, 0.0
    ).astype(BF16)
    for r in range(slots):
        total = states[r][0]
        rows = [total[(2 * t + x) * count : (2 * t + x + 1) * count] for x in (0, 1) for t in (0, 1)]
        out[:, r, :] = lax.dot_general(
            jnp.concatenate(rows, axis=1).astype(BF16), order_lanes, NN, preferred_element_type=F32
        )


def join_kernel(pieces, matrix, out):
    coeffs = jnp.sum(pieces[...], axis=0)
    for i in range(out.shape[0]):
        out[i] = jnp.concatenate([matrix[i], coeffs], axis=1).astype(BF16)


def cycle_kernel(received, pick, out):
    values = received[...].astype(F32)
    coeffs = values[:, :, 2 * LANES :]
    coeffs = jnp.concatenate([coeffs, coeffs], axis=1).reshape(2 * LANES, LANES).astype(BF16)
    picks = pick[...]
    products = []
    for h in (0, 1):
        matrix = values[:, :, h * LANES : (h + 1) * LANES].reshape(LANES, LANES)
        at_slot = lax.dot_general(picks, coeffs[h * LANES : (h + 1) * LANES], NT, preferred_element_type=F32)
        products.append(matrix * at_slot)
    lane = lax.broadcasted_iota(jnp.int32, (8, 2 * LANES), 1)
    part = lane // 2 % 2 * 2 + lane // 4 % 2
    gather = jnp.where(part == lax.broadcasted_iota(jnp.int32, part.shape, 0), 1.0, 0.0).astype(BF16)

    def exact(dot, x):
        head = x.astype(BF16)
        return dot(head) + dot((x - head.astype(F32)).astype(BF16))

    by_slot = exact(
        lambda y: lax.dot_general(gather, y, NT, preferred_element_type=F32), jnp.concatenate(products, axis=1)
    )
    grads = exact(lambda y: lax.dot_general(y, picks, NN, preferred_element_type=F32), by_slot)
    out[...] = jnp.broadcast_to(grads[:4].astype(BF16)[None], out.shape)


def adjoint_kernel(grads, legendre, mixed, out):
    slots = grads.shape[0]
    width = out.shape[3]
    straight = grads[...].astype(F32).reshape(slots * 4, LANES)
    row = lax.broadcasted_iota(jnp.int32, straight.shape, 0) % 4
    up = pltpu.roll(straight, straight.shape[0] - 1, 0)
    down = pltpu.roll(straight, 1, 0)
    up3 = pltpu.roll(straight, straight.shape[0] - 3, 0)
    down3 = pltpu.roll(straight, 3, 0)
    twisted = jnp.where(row == 0, -up3, jnp.where(row == 1, up, jnp.where(row == 2, down, -down3)))
    sums = lax.dot_general(straight.astype(BF16), legendre[:width], NT, preferred_element_type=F32)
    sums = sums + lax.dot_general(twisted.astype(BF16), legendre[width:], NT, preferred_element_type=F32)
    for c in range(out.shape[0]):
        pairs = jnp.sum((sums * mixed[c]).reshape(slots // 2, 8, sums.shape[1]), axis=0)
        out[c, :, 0, :] = pairs[:4] + pairs[4:]


def body(
    comp_alms,
    legendre,
    inv_noise,
    beam_window,
    mixing,
    channel_of,
    m_orders,
    cycle_of,
    cycle_pixels,
):
    slots = channel_of.shape[0]
    orders = m_orders.shape[0]
    cycles = legendre.shape[3]
    comps, _, _, width = comp_alms.shape
    chan = functools.partial(lax.axis_index, "chan")
    blk = functools.partial(lax.axis_index, "blk")
    held = inv_noise.shape[2]
    tall = inv_noise.shape[3] // LANES
    noise = inv_noise.reshape(2, held, tall, LANES).transpose(0, 2, 1, 3).reshape(2 * tall * held, LANES)
    partial, legs, mixed, *made_of = pl.pallas_call(
        functools.partial(forward_kernel, chan=chan, blk=blk, slots=held),
        out_shape=[
            jax.ShapeDtypeStruct((slots, 4, cycles), F32),
            pltpu.VMEM((2 * width, cycles), BF16),
            pltpu.VMEM((comps, 4 * slots, width), F32),
            pltpu.VMEM(noise.shape, F32),
            pltpu.VMEM((orders, LANES), F32),
            pltpu.VMEM((held, LANES), F32),
            pltpu.VMEM((1, cycles), jnp.int32),
        ],
        in_specs=[ANY] * 10,
        out_specs=[VMEM] * 7,
        scratch_shapes=[
            pltpu.SMEM(channel_of.shape, jnp.int32),
            pltpu.SMEM(mixing.shape[::-1], F32),
            pltpu.SMEM(m_orders.shape, jnp.int32),
            pltpu.SMEM(cycle_of.shape, jnp.int32),
            pltpu.SMEM(cycle_pixels.shape, jnp.int32),
            pltpu.VMEM(comp_alms.shape, F32),
            pltpu.VMEM((beam_window.shape[0], width), F32),
            pltpu.VMEM((slots * 4, 2 * width), F32),
            pltpu.SemaphoreType.DMA((11,)),
        ],
        name="forward",
    )(
        channel_of, mixing.T, m_orders, cycle_of, cycle_pixels, cycle_of.reshape(1, -1),
        comp_alms, beam_window, legendre, noise,
    )
    pieces = move(partial, "chan")
    weights, order_rows, numbers, cycle_row = map(in_vmem, made_of)
    matrix, pick = pl.pallas_call(
        cycle_matrix_kernel,
        out_shape=[pltpu.VMEM((orders, held, 2 * LANES), F32), pltpu.VMEM((cycles, LANES), BF16)],
        in_specs=[VMEM] * 4,
        out_specs=[VMEM] * 2,
        scratch_shapes=[pltpu.VMEM((held, 2, tall, LANES), F32)],
        name="matrices",
    )(order_rows, numbers, cycle_row, weights)
    message = pl.pallas_call(
        join_kernel,
        out_shape=pltpu.VMEM((orders, held, 3 * LANES), BF16),
        in_specs=[VMEM] * 2,
        out_specs=VMEM,
        name="join",
    )(in_vmem(pieces), in_vmem(matrix))
    grads = pl.pallas_call(
        cycle_kernel,
        out_shape=pltpu.VMEM((slots, 4, cycles), BF16),
        in_specs=[VMEM] * 2,
        out_specs=VMEM,
        name="cycles",
    )(in_vmem(move(message, "blk")), in_vmem(pick))
    return pl.pallas_call(
        adjoint_kernel,
        out_shape=jax.ShapeDtypeStruct(comp_alms.shape, F32),
        in_specs=[VMEM] * 3,
        out_specs=VMEM,
        name="adjoint",
    )(in_vmem(move(grads, "chan")), in_vmem(legs), in_vmem(mixed))


def solution(mesh):
    placed = (
        P(None, None, "blk", "chan"),
        P(None, "blk", None, None),
        P("chan", None, "blk", None),
        P(),
        P(),
        P(),
        P(),
        P(),
        P(),
    )
    return jax.shard_map(
        body, mesh=mesh, in_specs=placed, out_specs=P(None, None, "blk", "chan"), check_vma=False
    )
```

```python
import functools

import jax
import jax.numpy as jnp
from jax import lax
from jax.experimental import pallas as pl
from jax.experimental.pallas import tpu as pltpu
from jax.sharding import PartitionSpec as P

F32 = jnp.float32
BF16 = jnp.bfloat16
LANES = 128
NT = (((1,), (1,)), ((), ()))
NN = (((1,), (0,)), ((), ()))
COS = (0.9999999887921183, -19.739204415555925, 64.93911321613162, -85.45006149635309,
       60.16698573653733, -25.965151588112157, 6.525190124026944)
SIN = (6.28318530240345, -41.341700371179485, 81.60512965170976, -76.70298335354587,
       42.02566158843437, -14.898837201069828, 3.2367039052082127)

VMEM = pl.BlockSpec(memory_space=pltpu.VMEM)
ANY = pl.BlockSpec(memory_space=pl.ANY)


FLIP = {"chan": 8, "blk": 18}


def move(x, axis):
    members = [j ^ FLIP[axis] for j in range(x.shape[0])]
    return lax.all_to_all(x, axis, 0, 0, tiled=True, axis_index_groups=[members])


def in_vmem(x):
    return pltpu.with_memory_space_constraint(x, pltpu.VMEM)


def nearest(x):
    return jnp.floor(x + 0.5)


def poly(z, terms):
    total = jnp.full_like(z, terms[-1])
    for term in terms[-2::-1]:
        total = total * z + term
    return total


def cos_turns(y):
    return poly(y * y, COS)


def sin_turns(y):
    return y * poly(y * y, SIN)


def turns_of(steps, period):
    inverse = 1.0 / period
    rest = steps - nearest(steps * inverse) * period
    return rest * inverse


def forward_kernel(
    chan_of_hbm, mixing_hbm, orders_hbm, cycle_of_hbm, cycle_pixels_hbm, cycle_row_hbm, comp, beam, legendre, noise,
    out, leg, mixed_out, noise_out, order_out, number_out, cycle_row_out,
    chan_of, mixing, orders, cycle_of, cycle_pixels, comp_s, beam_s, alm_s, sems, *, chan, blk, slots
):
    width = comp.shape[3]
    first = chan() * width
    copies = [
        pltpu.make_async_copy(beam.at[:, pl.ds(first, width)], beam_s, sems.at[0]),
        pltpu.make_async_copy(legendre.at[0, 0, pl.ds(first, width), :], leg.at[pl.ds(0, width)], sems.at[1]),
        pltpu.make_async_copy(legendre.at[1, 0, pl.ds(first, width), :], leg.at[pl.ds(width, width)], sems.at[2]),
        pltpu.make_async_copy(comp, comp_s, sems.at[3]),
        pltpu.make_async_copy(chan_of_hbm, chan_of, sems.at[4]),
        pltpu.make_async_copy(mixing_hbm, mixing, sems.at[5]),
        pltpu.make_async_copy(orders_hbm, orders, sems.at[6]),
        pltpu.make_async_copy(cycle_of_hbm, cycle_of, sems.at[7]),
        pltpu.make_async_copy(cycle_pixels_hbm, cycle_pixels, sems.at[8]),
        pltpu.make_async_copy(cycle_row_hbm, cycle_row_out, sems.at[9]),
        pltpu.make_async_copy(noise, noise_out, sems.at[10]),
    ]
    for n in (4, 5, 6, 3, 0, 1, 2, 7, 8, 9, 10):
        copies[n].start()
    degrees = first + lax.broadcasted_iota(jnp.int32, (1, width), 1)
    for n in (4, 5, 6, 3, 0):
        copies[n].wait()
    order = orders[blk()]
    keep = jnp.where(degrees >= order, 1.0, 0.0)
    parts = [comp_s[c, :, 0, :] for c in range(comp.shape[0])]
    for k in range(out.shape[0]):
        channel = chan_of[k ^ FLIP["chan"]]
        row = beam_s[pl.ds(channel, 1), :] * keep
        mixed = mixing[0, channel] * parts[0]
        for c in range(1, len(parts)):
            mixed = mixed + mixing[c, channel] * parts[c]
        alm = mixed * row
        twisted = jnp.concatenate([-alm[3:4], alm[2:3], alm[1:2], -alm[0:1]], axis=0)
        alm_s[4 * k : 4 * k + 4, :width] = alm
        alm_s[4 * k : 4 * k + 4, width:] = twisted
        for c in range(len(parts)):
            mixed_out[c, 4 * k : 4 * k + 4, :] = jnp.broadcast_to(mixing[c, channel] * row, (4, width))
    copies[1].wait()
    copies[2].wait()
    sums = lax.dot_general(alm_s[...].astype(BF16), leg[...], NN, preferred_element_type=F32)
    out[...] = sums.reshape(out.shape)
    for i in range(orders.shape[0]):
        order_out[i : i + 1, :] = jnp.full((1, LANES), orders[i], jnp.int32).astype(F32)
    for copy in copies[7:]:
        copy.wait()
    start = blk() * slots
    for r in range(slots):
        number_out[r : r + 1, :] = jnp.full((1, LANES), cycle_pixels[cycle_of[start + r]], jnp.int32).astype(F32)


def cycle_matrix_kernel(order_rows, numbers, cycle_row, noise, out, pick_out, weight_s):
    count = order_rows.shape[0]
    slots = out.shape[1]
    square = (LANES, LANES)
    row = lax.broadcasted_iota(jnp.int32, square, 0)
    same = jnp.where(row == lax.broadcasted_iota(jnp.int32, square, 1) ^ (slots * FLIP["blk"]), 1.0, 0.0).astype(BF16)
    at_cycle = jnp.where(row == cycle_row[...], 1.0, 0.0).astype(BF16)
    pick_out[...] = lax.dot_general(same, at_cycle, NT, preferred_element_type=F32).astype(BF16)
    m = order_rows[...]
    odd_steps = (2 * lax.broadcasted_iota(jnp.int32, (count, LANES), 1) + 1).astype(F32) * m
    half = noise.shape[0] // 2
    tall = half // slots
    pixel = (
        lax.broadcasted_iota(jnp.int32, (tall, LANES), 0) * LANES
        + lax.broadcasted_iota(jnp.int32, (tall, LANES), 1)
    ).astype(F32)
    turns, states = [], []
    for r in range(slots):
        number = numbers[r : r + 1, :]
        live = jnp.where(pixel < number, 1.0 / number, 0.0)
        weight_s[r, 0] = noise[pl.ds(r, tall, stride=slots), :] * live
        weight_s[r, 1] = noise[pl.ds(half + r, tall, stride=slots), :] * live
        turn = turns_of(m * 32.0, number * 0.25)
        turn = turn - nearest(turn)
        turns.append((cos_turns(turn), sin_turns(turn)))
        base = turns_of(odd_steps, number * 2.0)
        base = base - nearest(base)
        states.append((jnp.zeros((4 * count, 2 * count), F32), cos_turns(base), sin_turns(base)))

    for even in range(0, tall, 2):
        for r in range(slots):
            total, c, s = states[r]
            turn_cos, turn_sin = turns[r]
            phases, weighted = [], []
            for step in (even, even + 1):
                q, u = (weight_s[r, t, step : step + 1, :] for t in (0, 1))
                phases.append(jnp.concatenate([c, s], axis=0).astype(BF16))
                weighted.append(jnp.concatenate([q * c, q * s, u * c, u * s], axis=0).astype(BF16))
                c, s = c * turn_cos - s * turn_sin, s * turn_cos + c * turn_sin
            total = total + lax.dot_general(
                jnp.concatenate(weighted, axis=1),
                jnp.concatenate(phases, axis=1),
                NT,
                preferred_element_type=F32,
            )
            states[r] = (total, c, s)

    source = lax.broadcasted_iota(jnp.int32, (2 * LANES, 1), 0)
    x, t, xx, ii = source // 128, source // 64 % 2, source // 32 % 2, source % 32 ^ FLIP["blk"]
    target = (ii // 16) * 128 + (ii % 16) * 8 + x * 4 + t * 2 + xx
    value = jnp.where(x == xx, 1.0, -1.0)
    order_lanes = jnp.where(
        lax.broadcasted_iota(jnp.int32, (2 * LANES, 2 * LANES), 1) == target, value, 0.0
    ).astype(BF16)
    for r in range(slots):
        total = states[r][0]
        rows = [total[(2 * t + x) * count : (2 * t + x + 1) * count] for x in (0, 1) for t in (0, 1)]
        out[:, r, :] = lax.dot_general(
            jnp.concatenate(rows, axis=1).astype(BF16), order_lanes, NN, preferred_element_type=F32
        )


def join_kernel(pieces, matrix, out):
    coeffs = jnp.sum(pieces[...], axis=0)
    for i in range(out.shape[0]):
        out[i] = jnp.concatenate([matrix[i ^ FLIP["blk"]], coeffs], axis=1).astype(BF16)


def cycle_kernel(received, pick, out):
    values = received[...].astype(F32)
    coeffs = values[:, :, 2 * LANES :]
    coeffs = jnp.concatenate([coeffs, coeffs], axis=1).reshape(2 * LANES, LANES).astype(BF16)
    picks = pick[...]
    products = []
    for h in (0, 1):
        matrix = values[:, :, h * LANES : (h + 1) * LANES].reshape(LANES, LANES)
        at_slot = lax.dot_general(picks, coeffs[h * LANES : (h + 1) * LANES], NT, preferred_element_type=F32)
        products.append(matrix * at_slot)
    lane = lax.broadcasted_iota(jnp.int32, (8, 2 * LANES), 1)
    part = lane // 2 % 2 * 2 + lane // 4 % 2
    gather = jnp.where(part == lax.broadcasted_iota(jnp.int32, part.shape, 0), 1.0, 0.0).astype(BF16)

    def exact(dot, x):
        head = x.astype(BF16)
        return dot(head) + dot((x - head.astype(F32)).astype(BF16))

    by_slot = exact(
        lambda y: lax.dot_general(gather, y, NT, preferred_element_type=F32), jnp.concatenate(products, axis=1)
    )
    grads = exact(lambda y: lax.dot_general(y, picks, NN, preferred_element_type=F32), by_slot)
    out[...] = jnp.broadcast_to(grads[:4].astype(BF16)[None], out.shape)


def adjoint_kernel(grads, legendre, mixed, out):
    slots = grads.shape[0]
    width = out.shape[3]
    straight = grads[...].astype(F32).reshape(slots * 4, LANES)
    row = lax.broadcasted_iota(jnp.int32, straight.shape, 0) % 4
    up = pltpu.roll(straight, straight.shape[0] - 1, 0)
    down = pltpu.roll(straight, 1, 0)
    up3 = pltpu.roll(straight, straight.shape[0] - 3, 0)
    down3 = pltpu.roll(straight, 3, 0)
    twisted = jnp.where(row == 0, -up3, jnp.where(row == 1, up, jnp.where(row == 2, down, -down3)))
    sums = lax.dot_general(straight.astype(BF16), legendre[:width], NT, preferred_element_type=F32)
    sums = sums + lax.dot_general(twisted.astype(BF16), legendre[width:], NT, preferred_element_type=F32)
    for c in range(out.shape[0]):
        pairs = jnp.sum((sums * mixed[c]).reshape(slots // 2, 8, sums.shape[1]), axis=0)
        out[c, :, 0, :] = pairs[:4] + pairs[4:]


def body(
    comp_alms,
    legendre,
    inv_noise,
    beam_window,
    mixing,
    channel_of,
    m_orders,
    cycle_of,
    cycle_pixels,
):
    slots = channel_of.shape[0]
    orders = m_orders.shape[0]
    cycles = legendre.shape[3]
    comps, _, _, width = comp_alms.shape
    chan = functools.partial(lax.axis_index, "chan")
    blk = functools.partial(lax.axis_index, "blk")
    held = inv_noise.shape[2]
    tall = inv_noise.shape[3] // LANES
    noise = inv_noise.reshape(2, held, tall, LANES).transpose(0, 2, 1, 3).reshape(2 * tall * held, LANES)
    partial, legs, mixed, *made_of = pl.pallas_call(
        functools.partial(forward_kernel, chan=chan, blk=blk, slots=held),
        out_shape=[
            jax.ShapeDtypeStruct((slots, 4, cycles), F32),
            pltpu.VMEM((2 * width, cycles), BF16),
            pltpu.VMEM((comps, 4 * slots, width), F32),
            pltpu.VMEM(noise.shape, F32),
            pltpu.VMEM((orders, LANES), F32),
            pltpu.VMEM((held, LANES), F32),
            pltpu.VMEM((1, cycles), jnp.int32),
        ],
        in_specs=[ANY] * 10,
        out_specs=[VMEM] * 7,
        scratch_shapes=[
            pltpu.SMEM(channel_of.shape, jnp.int32),
            pltpu.SMEM(mixing.shape[::-1], F32),
            pltpu.SMEM(m_orders.shape, jnp.int32),
            pltpu.SMEM(cycle_of.shape, jnp.int32),
            pltpu.SMEM(cycle_pixels.shape, jnp.int32),
            pltpu.VMEM(comp_alms.shape, F32),
            pltpu.VMEM((beam_window.shape[0], width), F32),
            pltpu.VMEM((slots * 4, 2 * width), F32),
            pltpu.SemaphoreType.DMA((11,)),
        ],
        name="forward",
    )(
        channel_of, mixing.T, m_orders, cycle_of, cycle_pixels, cycle_of.reshape(1, -1),
        comp_alms, beam_window, legendre, noise,
    )
    pieces = move(partial, "chan")
    weights, order_rows, numbers, cycle_row = map(in_vmem, made_of)
    matrix, pick = pl.pallas_call(
        cycle_matrix_kernel,
        out_shape=[pltpu.VMEM((orders, held, 2 * LANES), F32), pltpu.VMEM((cycles, LANES), BF16)],
        in_specs=[VMEM] * 4,
        out_specs=[VMEM] * 2,
        scratch_shapes=[pltpu.VMEM((held, 2, tall, LANES), F32)],
        name="matrices",
    )(order_rows, numbers, cycle_row, weights)
    message = pl.pallas_call(
        join_kernel,
        out_shape=pltpu.VMEM((orders, held, 3 * LANES), BF16),
        in_specs=[VMEM] * 2,
        out_specs=VMEM,
        name="join",
    )(in_vmem(pieces), in_vmem(matrix))
    grads = pl.pallas_call(
        cycle_kernel,
        out_shape=pltpu.VMEM((slots, 4, cycles), BF16),
        in_specs=[VMEM] * 2,
        out_specs=VMEM,
        name="cycles",
    )(in_vmem(move(message, "blk")), in_vmem(pick))
    return pl.pallas_call(
        adjoint_kernel,
        out_shape=jax.ShapeDtypeStruct(comp_alms.shape, F32),
        in_specs=[VMEM] * 3,
        out_specs=VMEM,
        name="adjoint",
    )(in_vmem(move(grads, "chan")), in_vmem(legs), in_vmem(mixed))


def solution(mesh):
    placed = (
        P(None, None, "blk", "chan"),
        P(None, "blk", None, None),
        P("chan", None, "blk", None),
        P(),
        P(),
        P(),
        P(),
        P(),
        P(),
    )
    return jax.shard_map(
        body, mesh=mesh, in_specs=placed, out_specs=P(None, None, "blk", "chan"), check_vma=False
    )
```

```python
import functools

import jax
import jax.numpy as jnp
from jax import lax
from jax.experimental import pallas as pl
from jax.experimental.pallas import tpu as pltpu
from jax.sharding import PartitionSpec as P

F32 = jnp.float32
BF16 = jnp.bfloat16
LANES = 128
NT = (((1,), (1,)), ((), ()))
NN = (((1,), (0,)), ((), ()))
COS = (0.9999999887921183, -19.739204415555925, 64.93911321613162, -85.45006149635309,
       60.16698573653733, -25.965151588112157, 6.525190124026944)
SIN = (6.28318530240345, -41.341700371179485, 81.60512965170976, -76.70298335354587,
       42.02566158843437, -14.898837201069828, 3.2367039052082127)

VMEM = pl.BlockSpec(memory_space=pltpu.VMEM)
ANY = pl.BlockSpec(memory_space=pl.ANY)


FLIP = {"out": 11, "blk": 26, "home": 9}


def move(x, axis, leg):
    members = [j ^ FLIP[leg] for j in range(x.shape[0])]
    return lax.all_to_all(x, axis, 0, 0, tiled=True, axis_index_groups=[members])


def in_vmem(x):
    return pltpu.with_memory_space_constraint(x, pltpu.VMEM)


def nearest(x):
    return jnp.floor(x + 0.5)


def poly(z, terms):
    total = jnp.full_like(z, terms[-1])
    for term in terms[-2::-1]:
        total = total * z + term
    return total


def cos_turns(y):
    return poly(y * y, COS)


def sin_turns(y):
    return y * poly(y * y, SIN)


def turns_of(steps, period):
    inverse = 1.0 / period
    rest = steps - nearest(steps * inverse) * period
    return rest * inverse


def forward_kernel(
    chan_of_hbm, mixing_hbm, orders_hbm, cycle_of_hbm, cycle_pixels_hbm, cycle_row_hbm, comp, beam, legendre, noise,
    out, leg, mixed_out, noise_out, order_out, number_out, cycle_row_out,
    chan_of, mixing, orders, cycle_of, cycle_pixels, comp_s, beam_s, alm_s, sems, *, chan, blk, slots
):
    width = comp.shape[3]
    first = chan() * width
    copies = [
        pltpu.make_async_copy(beam.at[:, pl.ds(first, width)], beam_s, sems.at[0]),
        pltpu.make_async_copy(legendre.at[0, 0, pl.ds(first, width), :], leg.at[pl.ds(0, width)], sems.at[1]),
        pltpu.make_async_copy(legendre.at[1, 0, pl.ds(first, width), :], leg.at[pl.ds(width, width)], sems.at[2]),
        pltpu.make_async_copy(comp, comp_s, sems.at[3]),
        pltpu.make_async_copy(chan_of_hbm, chan_of, sems.at[4]),
        pltpu.make_async_copy(mixing_hbm, mixing, sems.at[5]),
        pltpu.make_async_copy(orders_hbm, orders, sems.at[6]),
        pltpu.make_async_copy(cycle_of_hbm, cycle_of, sems.at[7]),
        pltpu.make_async_copy(cycle_pixels_hbm, cycle_pixels, sems.at[8]),
        pltpu.make_async_copy(cycle_row_hbm, cycle_row_out, sems.at[9]),
        pltpu.make_async_copy(noise, noise_out, sems.at[10]),
    ]
    for n in (4, 5, 6, 3, 0, 1, 2, 7, 8, 9, 10):
        copies[n].start()
    degrees = first + lax.broadcasted_iota(jnp.int32, (1, width), 1)
    for n in (4, 5, 6, 3, 0):
        copies[n].wait()
    order = orders[blk()]
    keep = jnp.where(degrees >= order, 1.0, 0.0)
    parts = [comp_s[c, :, 0, :] for c in range(comp.shape[0])]
    for k in range(out.shape[0]):
        channel = chan_of[k ^ FLIP["out"]]
        row = beam_s[pl.ds(channel, 1), :] * keep
        mixed = mixing[0, channel] * parts[0]
        for c in range(1, len(parts)):
            mixed = mixed + mixing[c, channel] * parts[c]
        alm = mixed * row
        twisted = jnp.concatenate([-alm[3:4], alm[2:3], alm[1:2], -alm[0:1]], axis=0)
        alm_s[4 * k : 4 * k + 4, :width] = alm
        alm_s[4 * k : 4 * k + 4, width:] = twisted
        place = k ^ FLIP["out"] ^ FLIP["home"]
        for c in range(len(parts)):
            mixed_out[c, 4 * place : 4 * place + 4, :] = jnp.broadcast_to(mixing[c, channel] * row, (4, width))
    copies[1].wait()
    copies[2].wait()
    sums = lax.dot_general(alm_s[...].astype(BF16), leg[...], NN, preferred_element_type=F32)
    out[...] = sums.reshape(out.shape)
    for i in range(orders.shape[0]):
        order_out[i : i + 1, :] = jnp.full((1, LANES), orders[i], jnp.int32).astype(F32)
    for copy in copies[7:]:
        copy.wait()
    start = blk() * slots
    for r in range(slots):
        number_out[r : r + 1, :] = jnp.full((1, LANES), cycle_pixels[cycle_of[start + r]], jnp.int32).astype(F32)


def cycle_matrix_kernel(order_rows, numbers, cycle_row, noise, out, pick_out, weight_s):
    count = order_rows.shape[0]
    slots = out.shape[1]
    square = (LANES, LANES)
    row = lax.broadcasted_iota(jnp.int32, square, 0)
    same = jnp.where(row == lax.broadcasted_iota(jnp.int32, square, 1) ^ (slots * FLIP["blk"]), 1.0, 0.0).astype(BF16)
    at_cycle = jnp.where(row == cycle_row[...], 1.0, 0.0).astype(BF16)
    pick_out[...] = lax.dot_general(same, at_cycle, NT, preferred_element_type=F32).astype(BF16)
    m = order_rows[...]
    odd_steps = (2 * lax.broadcasted_iota(jnp.int32, (count, LANES), 1) + 1).astype(F32) * m
    half = noise.shape[0] // 2
    tall = half // slots
    pixel = (
        lax.broadcasted_iota(jnp.int32, (tall, LANES), 0) * LANES
        + lax.broadcasted_iota(jnp.int32, (tall, LANES), 1)
    ).astype(F32)
    turns, states = [], []
    for r in range(slots):
        number = numbers[r : r + 1, :]
        live = jnp.where(pixel < number, 1.0 / number, 0.0)
        weight_s[r, 0] = noise[pl.ds(r, tall, stride=slots), :] * live
        weight_s[r, 1] = noise[pl.ds(half + r, tall, stride=slots), :] * live
        turn = turns_of(m * 32.0, number * 0.25)
        turn = turn - nearest(turn)
        turns.append((cos_turns(turn), sin_turns(turn)))
        base = turns_of(odd_steps, number * 2.0)
        base = base - nearest(base)
        states.append((jnp.zeros((4 * count, 2 * count), F32), cos_turns(base), sin_turns(base)))

    for even in range(0, tall, 2):
        for r in range(slots):
            total, c, s = states[r]
            turn_cos, turn_sin = turns[r]
            phases, weighted = [], []
            for step in (even, even + 1):
                q, u = (weight_s[r, t, step : step + 1, :] for t in (0, 1))
                phases.append(jnp.concatenate([c, s], axis=0).astype(BF16))
                weighted.append(jnp.concatenate([q * c, q * s, u * c, u * s], axis=0).astype(BF16))
                c, s = c * turn_cos - s * turn_sin, s * turn_cos + c * turn_sin
            total = total + lax.dot_general(
                jnp.concatenate(weighted, axis=1),
                jnp.concatenate(phases, axis=1),
                NT,
                preferred_element_type=F32,
            )
            states[r] = (total, c, s)

    source = lax.broadcasted_iota(jnp.int32, (2 * LANES, 1), 0)
    x, t, xx, ii = source // 128, source // 64 % 2, source // 32 % 2, source % 32 ^ FLIP["blk"]
    target = (ii // 16) * 128 + (ii % 16) * 8 + x * 4 + t * 2 + xx
    value = jnp.where(x == xx, 1.0, -1.0)
    order_lanes = jnp.where(
        lax.broadcasted_iota(jnp.int32, (2 * LANES, 2 * LANES), 1) == target, value, 0.0
    ).astype(BF16)
    for r in range(slots):
        total = states[r][0]
        rows = [total[(2 * t + x) * count : (2 * t + x + 1) * count] for x in (0, 1) for t in (0, 1)]
        out[:, r, :] = lax.dot_general(
            jnp.concatenate(rows, axis=1).astype(BF16), order_lanes, NN, preferred_element_type=F32
        )


def join_kernel(pieces, matrix, out):
    coeffs = jnp.sum(pieces[...], axis=0)
    for i in range(out.shape[0]):
        out[i] = jnp.concatenate([matrix[i ^ FLIP["blk"]], coeffs], axis=1).astype(BF16)


def cycle_kernel(received, pick, out):
    values = received[...].astype(F32)
    coeffs = values[:, :, 2 * LANES :]
    coeffs = jnp.concatenate([coeffs, coeffs], axis=1).reshape(2 * LANES, LANES).astype(BF16)
    picks = pick[...]
    products = []
    for h in (0, 1):
        matrix = values[:, :, h * LANES : (h + 1) * LANES].reshape(LANES, LANES)
        at_slot = lax.dot_general(picks, coeffs[h * LANES : (h + 1) * LANES], NT, preferred_element_type=F32)
        products.append(matrix * at_slot)
    lane = lax.broadcasted_iota(jnp.int32, (8, 2 * LANES), 1)
    part = lane // 2 % 2 * 2 + lane // 4 % 2
    gather = jnp.where(part == lax.broadcasted_iota(jnp.int32, part.shape, 0), 1.0, 0.0).astype(BF16)

    def exact(dot, x):
        head = x.astype(BF16)
        return dot(head) + dot((x - head.astype(F32)).astype(BF16))

    by_slot = exact(
        lambda y: lax.dot_general(gather, y, NT, preferred_element_type=F32), jnp.concatenate(products, axis=1)
    )
    grads = exact(lambda y: lax.dot_general(y, picks, NN, preferred_element_type=F32), by_slot)
    out[...] = jnp.broadcast_to(grads[:4].astype(BF16)[None], out.shape)


def adjoint_kernel(grads, legendre, mixed, out):
    slots = grads.shape[0]
    width = out.shape[3]
    straight = grads[...].astype(F32).reshape(slots * 4, LANES)
    row = lax.broadcasted_iota(jnp.int32, straight.shape, 0) % 4
    up = pltpu.roll(straight, straight.shape[0] - 1, 0)
    down = pltpu.roll(straight, 1, 0)
    up3 = pltpu.roll(straight, straight.shape[0] - 3, 0)
    down3 = pltpu.roll(straight, 3, 0)
    twisted = jnp.where(row == 0, -up3, jnp.where(row == 1, up, jnp.where(row == 2, down, -down3)))
    sums = lax.dot_general(straight.astype(BF16), legendre[:width], NT, preferred_element_type=F32)
    sums = sums + lax.dot_general(twisted.astype(BF16), legendre[width:], NT, preferred_element_type=F32)
    for c in range(out.shape[0]):
        pairs = jnp.sum((sums * mixed[c]).reshape(slots // 2, 8, sums.shape[1]), axis=0)
        out[c, :, 0, :] = pairs[:4] + pairs[4:]


def body(
    comp_alms,
    legendre,
    inv_noise,
    beam_window,
    mixing,
    channel_of,
    m_orders,
    cycle_of,
    cycle_pixels,
):
    slots = channel_of.shape[0]
    orders = m_orders.shape[0]
    cycles = legendre.shape[3]
    comps, _, _, width = comp_alms.shape
    chan = functools.partial(lax.axis_index, "chan")
    blk = functools.partial(lax.axis_index, "blk")
    held = inv_noise.shape[2]
    tall = inv_noise.shape[3] // LANES
    noise = inv_noise.reshape(2, held, tall, LANES).transpose(0, 2, 1, 3).reshape(2 * tall * held, LANES)
    partial, legs, mixed, *made_of = pl.pallas_call(
        functools.partial(forward_kernel, chan=chan, blk=blk, slots=held),
        out_shape=[
            jax.ShapeDtypeStruct((slots, 4, cycles), F32),
            pltpu.VMEM((2 * width, cycles), BF16),
            pltpu.VMEM((comps, 4 * slots, width), F32),
            pltpu.VMEM(noise.shape, F32),
            pltpu.VMEM((orders, LANES), F32),
            pltpu.VMEM((held, LANES), F32),
            pltpu.VMEM((1, cycles), jnp.int32),
        ],
        in_specs=[ANY] * 10,
        out_specs=[VMEM] * 7,
        scratch_shapes=[
            pltpu.SMEM(channel_of.shape, jnp.int32),
            pltpu.SMEM(mixing.shape[::-1], F32),
            pltpu.SMEM(m_orders.shape, jnp.int32),
            pltpu.SMEM(cycle_of.shape, jnp.int32),
            pltpu.SMEM(cycle_pixels.shape, jnp.int32),
            pltpu.VMEM(comp_alms.shape, F32),
            pltpu.VMEM((beam_window.shape[0], width), F32),
            pltpu.VMEM((slots * 4, 2 * width), F32),
            pltpu.SemaphoreType.DMA((11,)),
        ],
        name="forward",
    )(
        channel_of, mixing.T, m_orders, cycle_of, cycle_pixels, cycle_of.reshape(1, -1),
        comp_alms, beam_window, legendre, noise,
    )
    pieces = move(partial, "chan", "out")
    weights, order_rows, numbers, cycle_row = map(in_vmem, made_of)
    matrix, pick = pl.pallas_call(
        cycle_matrix_kernel,
        out_shape=[pltpu.VMEM((orders, held, 2 * LANES), F32), pltpu.VMEM((cycles, LANES), BF16)],
        in_specs=[VMEM] * 4,
        out_specs=[VMEM] * 2,
        scratch_shapes=[pltpu.VMEM((held, 2, tall, LANES), F32)],
        name="matrices",
    )(order_rows, numbers, cycle_row, weights)
    message = pl.pallas_call(
        join_kernel,
        out_shape=pltpu.VMEM((orders, held, 3 * LANES), BF16),
        in_specs=[VMEM] * 2,
        out_specs=VMEM,
        name="join",
    )(in_vmem(pieces), in_vmem(matrix))
    grads = pl.pallas_call(
        cycle_kernel,
        out_shape=pltpu.VMEM((slots, 4, cycles), BF16),
        in_specs=[VMEM] * 2,
        out_specs=VMEM,
        name="cycles",
    )(in_vmem(move(message, "blk", "blk")), in_vmem(pick))
    return pl.pallas_call(
        adjoint_kernel,
        out_shape=jax.ShapeDtypeStruct(comp_alms.shape, F32),
        in_specs=[VMEM] * 3,
        out_specs=VMEM,
        name="adjoint",
    )(in_vmem(move(grads, "chan", "home")), in_vmem(legs), in_vmem(mixed))


def solution(mesh):
    placed = (
        P(None, None, "blk", "chan"),
        P(None, "blk", None, None),
        P("chan", None, "blk", None),
        P(),
        P(),
        P(),
        P(),
        P(),
        P(),
    )
    return jax.shard_map(
        body, mesh=mesh, in_specs=placed, out_specs=P(None, None, "blk", "chan"), check_vma=False
    )
```

```python
import functools

import jax
import jax.numpy as jnp
from jax import lax
from jax.experimental import pallas as pl
from jax.experimental.pallas import tpu as pltpu
from jax.sharding import PartitionSpec as P

F32 = jnp.float32
BF16 = jnp.bfloat16
LANES = 128
NT = (((1,), (1,)), ((), ()))
NN = (((1,), (0,)), ((), ()))
COS = (0.9999999887921183, -19.739204415555925, 64.93911321613162, -85.45006149635309,
       60.16698573653733, -25.965151588112157, 6.525190124026944)
SIN = (6.28318530240345, -41.341700371179485, 81.60512965170976, -76.70298335354587,
       42.02566158843437, -14.898837201069828, 3.2367039052082127)

VMEM = pl.BlockSpec(memory_space=pltpu.VMEM)
ANY = pl.BlockSpec(memory_space=pl.ANY)


FLIP = {"out": 11, "blk": 26, "home": 9}


def move(x, axis, leg):
    members = [j ^ FLIP[leg] for j in range(x.shape[0])]
    return lax.all_to_all(x, axis, 0, 0, tiled=True, axis_index_groups=[members])


def in_vmem(x):
    return pltpu.with_memory_space_constraint(x, pltpu.VMEM)


def nearest(x):
    return jnp.floor(x + 0.5)


def poly(z, terms):
    total = jnp.full_like(z, terms[-1])
    for term in terms[-2::-1]:
        total = total * z + term
    return total


def cos_turns(y):
    return poly(y * y, COS)


def sin_turns(y):
    return y * poly(y * y, SIN)


def turns_of(steps, period):
    inverse = 1.0 / period
    rest = steps - nearest(steps * inverse) * period
    return rest * inverse


def forward_kernel(
    chan_of_hbm, mixing_hbm, orders_hbm, cycle_of_hbm, cycle_pixels_hbm, cycle_row_hbm, comp, beam, legendre, noise,
    out, leg, mixed_out, noise_out, order_out, number_out, cycle_row_out,
    chan_of, mixing, orders, cycle_of, cycle_pixels, comp_s, beam_s, alm_s, sems, *, chan, blk, slots
):
    width = comp.shape[3]
    first = chan() * width
    copies = [
        pltpu.make_async_copy(beam.at[:, pl.ds(first, width)], beam_s, sems.at[0]),
        pltpu.make_async_copy(legendre.at[0, 0, pl.ds(first, width), :], leg.at[pl.ds(0, width)], sems.at[1]),
        pltpu.make_async_copy(legendre.at[1, 0, pl.ds(first, width), :], leg.at[pl.ds(width, width)], sems.at[2]),
        pltpu.make_async_copy(comp, comp_s, sems.at[3]),
        pltpu.make_async_copy(chan_of_hbm, chan_of, sems.at[4]),
        pltpu.make_async_copy(mixing_hbm, mixing, sems.at[5]),
        pltpu.make_async_copy(orders_hbm, orders, sems.at[6]),
        pltpu.make_async_copy(cycle_of_hbm, cycle_of, sems.at[7]),
        pltpu.make_async_copy(cycle_pixels_hbm, cycle_pixels, sems.at[8]),
        pltpu.make_async_copy(cycle_row_hbm, cycle_row_out, sems.at[9]),
        pltpu.make_async_copy(noise, noise_out, sems.at[10]),
    ]
    for n in (4, 5, 6, 3, 0, 1, 2, 7, 8, 9, 10):
        copies[n].start()
    degrees = first + lax.broadcasted_iota(jnp.int32, (1, width), 1)
    for n in (4, 5, 6, 3, 0):
        copies[n].wait()
    order = orders[blk()]
    keep = jnp.where(degrees >= order, 1.0, 0.0)
    parts = [comp_s[c, :, 0, :] for c in range(comp.shape[0])]
    for k in range(out.shape[0]):
        channel = chan_of[k ^ FLIP["out"]]
        row = beam_s[pl.ds(channel, 1), :] * keep
        mixed = mixing[0, channel] * parts[0]
        for c in range(1, len(parts)):
            mixed = mixed + mixing[c, channel] * parts[c]
        alm = mixed * row
        twisted = jnp.concatenate([-alm[3:4], alm[2:3], alm[1:2], -alm[0:1]], axis=0)
        alm_s[4 * k : 4 * k + 4, :width] = alm
        alm_s[4 * k : 4 * k + 4, width:] = twisted
        place = k ^ FLIP["out"] ^ FLIP["home"]
        for c in range(len(parts)):
            mixed_out[c, 4 * place : 4 * place + 4, :] = jnp.broadcast_to(mixing[c, channel] * row, (4, width))
    copies[1].wait()
    copies[2].wait()
    sums = lax.dot_general(alm_s[...].astype(BF16), leg[...], NN, preferred_element_type=F32)
    out[...] = sums.reshape(out.shape)
    for i in range(orders.shape[0]):
        order_out[i : i + 1, :] = jnp.full((1, LANES), orders[i], jnp.int32).astype(F32)
    for copy in copies[7:]:
        copy.wait()
    start = blk() * slots
    for r in range(slots):
        number_out[r : r + 1, :] = jnp.full((1, LANES), cycle_pixels[cycle_of[start + r]], jnp.int32).astype(F32)


def cycle_matrix_kernel(order_rows, numbers, cycle_row, noise, out, pick_out, weight_s):
    count = order_rows.shape[0]
    slots = out.shape[1]
    square = (LANES, LANES)
    row = lax.broadcasted_iota(jnp.int32, square, 0)
    same = jnp.where(row == lax.broadcasted_iota(jnp.int32, square, 1) ^ (slots * FLIP["blk"]), 1.0, 0.0).astype(BF16)
    at_cycle = jnp.where(row == cycle_row[...], 1.0, 0.0).astype(BF16)
    pick_out[...] = lax.dot_general(same, at_cycle, NT, preferred_element_type=F32).astype(BF16)
    m = order_rows[...]
    odd_steps = (2 * lax.broadcasted_iota(jnp.int32, (count, LANES), 1) + 1).astype(F32) * m
    half = noise.shape[0] // 2
    tall = half // slots
    pixel = (
        lax.broadcasted_iota(jnp.int32, (tall, LANES), 0) * LANES
        + lax.broadcasted_iota(jnp.int32, (tall, LANES), 1)
    ).astype(F32)
    turns, states = [], []
    for r in range(slots):
        number = numbers[r : r + 1, :]
        live = jnp.where(pixel < number, 1.0 / number, 0.0)
        weight_s[r, 0] = noise[pl.ds(r, tall, stride=slots), :] * live
        weight_s[r, 1] = noise[pl.ds(half + r, tall, stride=slots), :] * live
        turn = turns_of(m * 32.0, number * 0.25)
        turn = turn - nearest(turn)
        turns.append((cos_turns(turn), sin_turns(turn)))
        base = turns_of(odd_steps, number * 2.0)
        base = base - nearest(base)
        states.append((jnp.zeros((4 * count, 2 * count), F32), cos_turns(base), sin_turns(base)))

    for even in range(0, tall, 2):
        for r in range(slots):
            total, c, s = states[r]
            turn_cos, turn_sin = turns[r]
            phases, weighted = [], []
            for step in (even, even + 1):
                q, u = (weight_s[r, t, step : step + 1, :] for t in (0, 1))
                phases.append(jnp.concatenate([c, s], axis=0).astype(BF16))
                weighted.append(jnp.concatenate([q * c, q * s, u * c, u * s], axis=0).astype(BF16))
                c, s = c * turn_cos - s * turn_sin, s * turn_cos + c * turn_sin
            total = total + lax.dot_general(
                jnp.concatenate(weighted, axis=1),
                jnp.concatenate(phases, axis=1),
                NT,
                preferred_element_type=F32,
            )
            states[r] = (total, c, s)

    source = lax.broadcasted_iota(jnp.int32, (2 * LANES, 1), 0)
    x, t, xx, ii = source // 128, source // 64 % 2, source // 32 % 2, source % 32 ^ FLIP["blk"]
    target = (ii // 16) * 128 + (ii % 16) * 8 + x * 4 + t * 2 + xx
    value = jnp.where(x == xx, 1.0, -1.0)
    order_lanes = jnp.where(
        lax.broadcasted_iota(jnp.int32, (2 * LANES, 2 * LANES), 1) == target, value, 0.0
    ).astype(BF16)
    for r in range(slots):
        total = states[r][0]
        rows = [total[(2 * t + x) * count : (2 * t + x + 1) * count] for x in (0, 1) for t in (0, 1)]
        out[:, r, :] = lax.dot_general(
            jnp.concatenate(rows, axis=1).astype(BF16), order_lanes, NN, preferred_element_type=F32
        )


def join_kernel(pieces, matrix, out):
    coeffs = jnp.sum(pieces[...], axis=0)
    for i in range(out.shape[0]):
        out[i] = jnp.concatenate([matrix[i ^ FLIP["blk"]], coeffs], axis=1).astype(BF16)


def cycle_kernel(received, pick, out):
    values = received[...].astype(F32)
    coeffs = values[:, :, 2 * LANES :]
    coeffs = jnp.concatenate([coeffs, coeffs], axis=1).reshape(2 * LANES, LANES).astype(BF16)
    picks = pick[...]
    products = []
    for h in (0, 1):
        matrix = values[:, :, h * LANES : (h + 1) * LANES].reshape(LANES, LANES)
        at_slot = lax.dot_general(picks, coeffs[h * LANES : (h + 1) * LANES], NT, preferred_element_type=F32)
        products.append(matrix * at_slot)
    lane = lax.broadcasted_iota(jnp.int32, (8, 2 * LANES), 1)
    part = lane // 2 % 2 * 2 + lane // 4 % 2
    gather = jnp.where(part == lax.broadcasted_iota(jnp.int32, part.shape, 0), 1.0, 0.0).astype(BF16)

    def exact(dot, x):
        head = x.astype(BF16)
        return dot(head) + dot((x - head.astype(F32)).astype(BF16))

    by_slot = exact(
        lambda y: lax.dot_general(gather, y, NT, preferred_element_type=F32), jnp.concatenate(products, axis=1)
    )
    grads = exact(lambda y: lax.dot_general(y, picks, NN, preferred_element_type=F32), by_slot)
    out[...] = jnp.broadcast_to(grads[:4].astype(BF16)[None], out.shape)


def adjoint_kernel(grads, legendre, mixed, out):
    slots = grads.shape[0]
    width = out.shape[3]
    straight = grads[...].astype(F32).reshape(slots * 4, LANES)
    row = lax.broadcasted_iota(jnp.int32, straight.shape, 0) % 4
    up = pltpu.roll(straight, straight.shape[0] - 1, 0)
    down = pltpu.roll(straight, 1, 0)
    up3 = pltpu.roll(straight, straight.shape[0] - 3, 0)
    down3 = pltpu.roll(straight, 3, 0)
    twisted = jnp.where(row == 0, -up3, jnp.where(row == 1, up, jnp.where(row == 2, down, -down3)))
    sums = lax.dot_general(
        jnp.concatenate([straight, twisted], axis=1).astype(BF16),
        jnp.concatenate([legendre[:width], legendre[width:]], axis=1),
        NT,
        preferred_element_type=F32,
    )
    for c in range(out.shape[0]):
        pairs = jnp.sum((sums * mixed[c]).reshape(slots // 2, 8, sums.shape[1]), axis=0)
        out[c, :, 0, :] = pairs[:4] + pairs[4:]


def body(
    comp_alms,
    legendre,
    inv_noise,
    beam_window,
    mixing,
    channel_of,
    m_orders,
    cycle_of,
    cycle_pixels,
):
    slots = channel_of.shape[0]
    orders = m_orders.shape[0]
    cycles = legendre.shape[3]
    comps, _, _, width = comp_alms.shape
    chan = functools.partial(lax.axis_index, "chan")
    blk = functools.partial(lax.axis_index, "blk")
    held = inv_noise.shape[2]
    tall = inv_noise.shape[3] // LANES
    noise = inv_noise.reshape(2, held, tall, LANES).transpose(0, 2, 1, 3).reshape(2 * tall * held, LANES)
    partial, legs, mixed, *made_of = pl.pallas_call(
        functools.partial(forward_kernel, chan=chan, blk=blk, slots=held),
        out_shape=[
            jax.ShapeDtypeStruct((slots, 4, cycles), F32),
            pltpu.VMEM((2 * width, cycles), BF16),
            pltpu.VMEM((comps, 4 * slots, width), F32),
            pltpu.VMEM(noise.shape, F32),
            pltpu.VMEM((orders, LANES), F32),
            pltpu.VMEM((held, LANES), F32),
            pltpu.VMEM((1, cycles), jnp.int32),
        ],
        in_specs=[ANY] * 10,
        out_specs=[VMEM] * 7,
        scratch_shapes=[
            pltpu.SMEM(channel_of.shape, jnp.int32),
            pltpu.SMEM(mixing.shape[::-1], F32),
            pltpu.SMEM(m_orders.shape, jnp.int32),
            pltpu.SMEM(cycle_of.shape, jnp.int32),
            pltpu.SMEM(cycle_pixels.shape, jnp.int32),
            pltpu.VMEM(comp_alms.shape, F32),
            pltpu.VMEM((beam_window.shape[0], width), F32),
            pltpu.VMEM((slots * 4, 2 * width), F32),
            pltpu.SemaphoreType.DMA((11,)),
        ],
        name="forward",
    )(
        channel_of, mixing.T, m_orders, cycle_of, cycle_pixels, cycle_of.reshape(1, -1),
        comp_alms, beam_window, legendre, noise,
    )
    pieces = move(partial, "chan", "out")
    weights, order_rows, numbers, cycle_row = map(in_vmem, made_of)
    matrix, pick = pl.pallas_call(
        cycle_matrix_kernel,
        out_shape=[pltpu.VMEM((orders, held, 2 * LANES), F32), pltpu.VMEM((cycles, LANES), BF16)],
        in_specs=[VMEM] * 4,
        out_specs=[VMEM] * 2,
        scratch_shapes=[pltpu.VMEM((held, 2, tall, LANES), F32)],
        name="matrices",
    )(order_rows, numbers, cycle_row, weights)
    message = pl.pallas_call(
        join_kernel,
        out_shape=pltpu.VMEM((orders, held, 3 * LANES), BF16),
        in_specs=[VMEM] * 2,
        out_specs=VMEM,
        name="join",
    )(in_vmem(pieces), in_vmem(matrix))
    grads = pl.pallas_call(
        cycle_kernel,
        out_shape=pltpu.VMEM((slots, 4, cycles), BF16),
        in_specs=[VMEM] * 2,
        out_specs=VMEM,
        name="cycles",
    )(in_vmem(move(message, "blk", "blk")), in_vmem(pick))
    return pl.pallas_call(
        adjoint_kernel,
        out_shape=jax.ShapeDtypeStruct(comp_alms.shape, F32),
        in_specs=[VMEM] * 3,
        out_specs=VMEM,
        name="adjoint",
    )(in_vmem(move(grads, "chan", "home")), in_vmem(legs), in_vmem(mixed))


def solution(mesh):
    placed = (
        P(None, None, "blk", "chan"),
        P(None, "blk", None, None),
        P("chan", None, "blk", None),
        P(),
        P(),
        P(),
        P(),
        P(),
        P(),
    )
    return jax.shard_map(
        body, mesh=mesh, in_specs=placed, out_specs=P(None, None, "blk", "chan"), check_vma=False
    )
```

```python
import functools

import jax
import jax.numpy as jnp
from jax import lax
from jax.experimental import pallas as pl
from jax.experimental.pallas import tpu as pltpu
from jax.sharding import PartitionSpec as P

F32 = jnp.float32
BF16 = jnp.bfloat16
LANES = 128
NT = (((1,), (1,)), ((), ()))
NN = (((1,), (0,)), ((), ()))
COS = (0.9999999887921183, -19.739204415555925, 64.93911321613162, -85.45006149635309,
       60.16698573653733, -25.965151588112157, 6.525190124026944)
SIN = (6.28318530240345, -41.341700371179485, 81.60512965170976, -76.70298335354587,
       42.02566158843437, -14.898837201069828, 3.2367039052082127)

VMEM = pl.BlockSpec(memory_space=pltpu.VMEM)
ANY = pl.BlockSpec(memory_space=pl.ANY)


FLIP = {"out": 11, "blk": 26, "home": 9}


def move(x, axis, leg):
    members = [j ^ FLIP[leg] for j in range(x.shape[0])]
    return lax.all_to_all(x, axis, 0, 0, tiled=True, axis_index_groups=[members])


def in_vmem(x):
    return pltpu.with_memory_space_constraint(x, pltpu.VMEM)


def nearest(x):
    return jnp.floor(x + 0.5)


def poly(z, terms):
    total = jnp.full_like(z, terms[-1])
    for term in terms[-2::-1]:
        total = total * z + term
    return total


def cos_turns(y):
    return poly(y * y, COS)


def sin_turns(y):
    return y * poly(y * y, SIN)


def turns_of(steps, period):
    inverse = 1.0 / period
    rest = steps - nearest(steps * inverse) * period
    return rest * inverse


def forward_kernel(
    chan_of_hbm, mixing_hbm, orders_hbm, cycle_of_hbm, cycle_pixels_hbm, cycle_row_hbm, comp, beam, legendre, noise,
    out, leg, mixed_out, noise_out, order_out, number_out, cycle_row_out,
    chan_of, mixing, orders, cycle_of, cycle_pixels, comp_s, beam_s, alm_s, sems, *, chan, blk, slots
):
    width = comp.shape[3]
    first = chan() * width
    copies = [
        pltpu.make_async_copy(beam.at[:, pl.ds(first, width)], beam_s, sems.at[0]),
        pltpu.make_async_copy(legendre.at[0, 0, pl.ds(first, width), :], leg.at[pl.ds(0, width)], sems.at[1]),
        pltpu.make_async_copy(legendre.at[1, 0, pl.ds(first, width), :], leg.at[pl.ds(width, width)], sems.at[2]),
        pltpu.make_async_copy(comp, comp_s, sems.at[3]),
        pltpu.make_async_copy(chan_of_hbm, chan_of, sems.at[4]),
        pltpu.make_async_copy(mixing_hbm, mixing, sems.at[5]),
        pltpu.make_async_copy(orders_hbm, orders, sems.at[6]),
        pltpu.make_async_copy(cycle_of_hbm, cycle_of, sems.at[7]),
        pltpu.make_async_copy(cycle_pixels_hbm, cycle_pixels, sems.at[8]),
        pltpu.make_async_copy(cycle_row_hbm, cycle_row_out, sems.at[9]),
        pltpu.make_async_copy(noise, noise_out, sems.at[10]),
    ]
    for n in (4, 5, 6, 3, 0, 1, 2, 7, 8, 9, 10):
        copies[n].start()
    degrees = first + lax.broadcasted_iota(jnp.int32, (1, width), 1)
    for n in (4, 5, 6, 3, 0):
        copies[n].wait()
    order = orders[blk()]
    keep = jnp.where(degrees >= order, 1.0, 0.0)
    parts = [comp_s[c, :, 0, :] for c in range(comp.shape[0])]
    for k in range(out.shape[0]):
        channel = chan_of[k ^ FLIP["out"]]
        row = beam_s[pl.ds(channel, 1), :] * keep
        mixed = mixing[0, channel] * parts[0]
        for c in range(1, len(parts)):
            mixed = mixed + mixing[c, channel] * parts[c]
        alm = mixed * row
        twisted = jnp.concatenate([-alm[3:4], alm[2:3], alm[1:2], -alm[0:1]], axis=0)
        alm_s[4 * k : 4 * k + 4, :width] = alm
        alm_s[4 * k : 4 * k + 4, width:] = twisted
        place = k ^ FLIP["out"] ^ FLIP["home"]
        for c in range(len(parts)):
            mixed_out[c, 4 * place : 4 * place + 4, :] = jnp.broadcast_to(mixing[c, channel] * row, (4, width))
    copies[1].wait()
    copies[2].wait()
    sums = lax.dot_general(alm_s[...].astype(BF16), leg[...], NN, preferred_element_type=F32)
    out[...] = sums.reshape(out.shape)
    for i in range(orders.shape[0]):
        order_out[i : i + 1, :] = jnp.full((1, LANES), orders[i], jnp.int32).astype(F32)
    for copy in copies[7:]:
        copy.wait()
    start = blk() * slots
    for r in range(slots):
        number_out[r : r + 1, :] = jnp.full((1, LANES), cycle_pixels[cycle_of[start + r]], jnp.int32).astype(F32)


def cycle_matrix_kernel(order_rows, numbers, cycle_row, noise, out, pick_out, weight_s):
    count = order_rows.shape[0]
    slots = out.shape[1]
    square = (LANES, LANES)
    row = lax.broadcasted_iota(jnp.int32, square, 0)
    same = jnp.where(row == lax.broadcasted_iota(jnp.int32, square, 1) ^ (slots * FLIP["blk"]), 1.0, 0.0).astype(BF16)
    at_cycle = jnp.where(row == cycle_row[...], 1.0, 0.0).astype(BF16)
    pick_out[...] = lax.dot_general(same, at_cycle, NT, preferred_element_type=F32).astype(BF16)
    m = order_rows[...]
    odd_steps = (2 * lax.broadcasted_iota(jnp.int32, (count, LANES), 1) + 1).astype(F32) * m
    half = noise.shape[0] // 2
    tall = half // slots
    pixel = (
        lax.broadcasted_iota(jnp.int32, (tall, LANES), 0) * LANES
        + lax.broadcasted_iota(jnp.int32, (tall, LANES), 1)
    ).astype(F32)
    turns, states = [], []
    for r in range(slots):
        number = numbers[r : r + 1, :]
        live = jnp.where(pixel < number, 1.0 / number, 0.0)
        weight_s[r, 0] = noise[pl.ds(r, tall, stride=slots), :] * live
        weight_s[r, 1] = noise[pl.ds(half + r, tall, stride=slots), :] * live
        turn = turns_of(m * 32.0, number * 0.25)
        turn = turn - nearest(turn)
        turns.append((cos_turns(turn), sin_turns(turn)))
        base = turns_of(odd_steps, number * 2.0)
        base = base - nearest(base)
        states.append((jnp.zeros((4 * count, 2 * count), F32), cos_turns(base), sin_turns(base)))

    for even in range(0, tall, 2):
        for r in range(slots):
            total, c, s = states[r]
            turn_cos, turn_sin = turns[r]
            phases, weighted = [], []
            for step in (even, even + 1):
                q, u = (weight_s[r, t, step : step + 1, :] for t in (0, 1))
                phases.append(jnp.concatenate([c, s], axis=0).astype(BF16))
                weighted.append(jnp.concatenate([q * c, q * s, u * c, u * s], axis=0).astype(BF16))
                c, s = c * turn_cos - s * turn_sin, s * turn_cos + c * turn_sin
            total = total + lax.dot_general(
                jnp.concatenate(weighted, axis=1),
                jnp.concatenate(phases, axis=1),
                NT,
                preferred_element_type=F32,
            )
            states[r] = (total, c, s)

    source = lax.broadcasted_iota(jnp.int32, (2 * LANES, 1), 0)
    x, t, xx, ii = source // 128, source // 64 % 2, source // 32 % 2, source % 32 ^ FLIP["blk"]
    target = (ii // 16) * 128 + (ii % 16) * 8 + x * 4 + t * 2 + xx
    value = jnp.where(x == xx, 1.0, -1.0)
    order_lanes = jnp.where(
        lax.broadcasted_iota(jnp.int32, (2 * LANES, 2 * LANES), 1) == target, value, 0.0
    ).astype(BF16)
    for r in range(slots):
        total = states[r][0]
        rows = [total[(2 * t + x) * count : (2 * t + x + 1) * count] for x in (0, 1) for t in (0, 1)]
        out[:, r, :] = lax.dot_general(
            jnp.concatenate(rows, axis=1).astype(BF16), order_lanes, NN, preferred_element_type=F32
        )


def join_kernel(pieces, matrix, out):
    coeffs = jnp.sum(pieces[...], axis=0)
    for i in range(out.shape[0]):
        out[i] = jnp.concatenate([matrix[i ^ FLIP["blk"]], coeffs], axis=1).astype(BF16)


def cycle_kernel(received, pick, out):
    values = received[...].astype(F32)
    coeffs = values[:, :, 2 * LANES :]
    coeffs = jnp.concatenate([coeffs, coeffs], axis=1).reshape(2 * LANES, LANES).astype(BF16)
    picks = pick[...]
    products = []
    for h in (0, 1):
        matrix = values[:, :, h * LANES : (h + 1) * LANES].reshape(LANES, LANES)
        at_slot = lax.dot_general(picks, coeffs[h * LANES : (h + 1) * LANES], NT, preferred_element_type=F32)
        products.append(matrix * at_slot)
    lane = lax.broadcasted_iota(jnp.int32, (8, 2 * LANES), 1)
    part = lane // 2 % 2 * 2 + lane // 4 % 2
    gather = jnp.where(part == lax.broadcasted_iota(jnp.int32, part.shape, 0), 1.0, 0.0).astype(BF16)

    def exact(dot, x):
        head = x.astype(BF16)
        return dot(head) + dot((x - head.astype(F32)).astype(BF16))

    by_slot = exact(
        lambda y: lax.dot_general(gather, y, NT, preferred_element_type=F32), jnp.concatenate(products, axis=1)
    )
    head = by_slot.astype(BF16).astype(F32)
    halves = jnp.concatenate([head, by_slot - head], axis=0).astype(BF16)
    halves = lax.dot_general(halves, picks, NN, preferred_element_type=F32)
    grads = halves[:8] + halves[8:]
    out[...] = jnp.broadcast_to(grads[:4].astype(BF16)[None], out.shape)


def adjoint_kernel(grads, legendre, mixed, out):
    slots = grads.shape[0]
    width = out.shape[3]
    straight = grads[...].astype(F32).reshape(slots * 4, LANES)
    row = lax.broadcasted_iota(jnp.int32, straight.shape, 0) % 4
    up = pltpu.roll(straight, straight.shape[0] - 1, 0)
    down = pltpu.roll(straight, 1, 0)
    up3 = pltpu.roll(straight, straight.shape[0] - 3, 0)
    down3 = pltpu.roll(straight, 3, 0)
    twisted = jnp.where(row == 0, -up3, jnp.where(row == 1, up, jnp.where(row == 2, down, -down3)))
    sums = lax.dot_general(
        jnp.concatenate([straight, twisted], axis=1).astype(BF16),
        jnp.concatenate([legendre[:width], legendre[width:]], axis=1),
        NT,
        preferred_element_type=F32,
    )
    for c in range(out.shape[0]):
        pairs = jnp.sum((sums * mixed[c]).reshape(slots // 2, 8, sums.shape[1]), axis=0)
        out[c, :, 0, :] = pairs[:4] + pairs[4:]


def body(
    comp_alms,
    legendre,
    inv_noise,
    beam_window,
    mixing,
    channel_of,
    m_orders,
    cycle_of,
    cycle_pixels,
):
    slots = channel_of.shape[0]
    orders = m_orders.shape[0]
    cycles = legendre.shape[3]
    comps, _, _, width = comp_alms.shape
    chan = functools.partial(lax.axis_index, "chan")
    blk = functools.partial(lax.axis_index, "blk")
    held = inv_noise.shape[2]
    tall = inv_noise.shape[3] // LANES
    noise = inv_noise.reshape(2, held, tall, LANES).transpose(0, 2, 1, 3).reshape(2 * tall * held, LANES)
    partial, legs, mixed, *made_of = pl.pallas_call(
        functools.partial(forward_kernel, chan=chan, blk=blk, slots=held),
        out_shape=[
            jax.ShapeDtypeStruct((slots, 4, cycles), F32),
            pltpu.VMEM((2 * width, cycles), BF16),
            pltpu.VMEM((comps, 4 * slots, width), F32),
            pltpu.VMEM(noise.shape, F32),
            pltpu.VMEM((orders, LANES), F32),
            pltpu.VMEM((held, LANES), F32),
            pltpu.VMEM((1, cycles), jnp.int32),
        ],
        in_specs=[ANY] * 10,
        out_specs=[VMEM] * 7,
        scratch_shapes=[
            pltpu.SMEM(channel_of.shape, jnp.int32),
            pltpu.SMEM(mixing.shape[::-1], F32),
            pltpu.SMEM(m_orders.shape, jnp.int32),
            pltpu.SMEM(cycle_of.shape, jnp.int32),
            pltpu.SMEM(cycle_pixels.shape, jnp.int32),
            pltpu.VMEM(comp_alms.shape, F32),
            pltpu.VMEM((beam_window.shape[0], width), F32),
            pltpu.VMEM((slots * 4, 2 * width), F32),
            pltpu.SemaphoreType.DMA((11,)),
        ],
        name="forward",
    )(
        channel_of, mixing.T, m_orders, cycle_of, cycle_pixels, cycle_of.reshape(1, -1),
        comp_alms, beam_window, legendre, noise,
    )
    pieces = move(partial, "chan", "out")
    weights, order_rows, numbers, cycle_row = map(in_vmem, made_of)
    matrix, pick = pl.pallas_call(
        cycle_matrix_kernel,
        out_shape=[pltpu.VMEM((orders, held, 2 * LANES), F32), pltpu.VMEM((cycles, LANES), BF16)],
        in_specs=[VMEM] * 4,
        out_specs=[VMEM] * 2,
        scratch_shapes=[pltpu.VMEM((held, 2, tall, LANES), F32)],
        name="matrices",
    )(order_rows, numbers, cycle_row, weights)
    message = pl.pallas_call(
        join_kernel,
        out_shape=pltpu.VMEM((orders, held, 3 * LANES), BF16),
        in_specs=[VMEM] * 2,
        out_specs=VMEM,
        name="join",
    )(in_vmem(pieces), in_vmem(matrix))
    grads = pl.pallas_call(
        cycle_kernel,
        out_shape=pltpu.VMEM((slots, 4, cycles), BF16),
        in_specs=[VMEM] * 2,
        out_specs=VMEM,
        name="cycles",
    )(in_vmem(move(message, "blk", "blk")), in_vmem(pick))
    return pl.pallas_call(
        adjoint_kernel,
        out_shape=jax.ShapeDtypeStruct(comp_alms.shape, F32),
        in_specs=[VMEM] * 3,
        out_specs=VMEM,
        name="adjoint",
    )(in_vmem(move(grads, "chan", "home")), in_vmem(legs), in_vmem(mixed))


def solution(mesh):
    placed = (
        P(None, None, "blk", "chan"),
        P(None, "blk", None, None),
        P("chan", None, "blk", None),
        P(),
        P(),
        P(),
        P(),
        P(),
        P(),
    )
    return jax.shard_map(
        body, mesh=mesh, in_specs=placed, out_specs=P(None, None, "blk", "chan"), check_vma=False
    )
```
